32 devices in a mesh: groups: 2 (over y), tensor: 4 (over z), dp: 4 (over x, core).
Axes of the slice: x: 2, y: 2, z: 4, core: 2. Of those that a mesh axis runs over, the one named last changes fastest.
Arguments:
- hidden_in: bfloat16 [512, 8192], P(('groups', 'dp'), 'tensor'), parts along dimension 0, may hold values from -6 to 6
- norm_gain: bfloat16 [8192], replicated, may hold values from 0.099609375 to 1.8984375
- w_query: bfloat16 [8192, 4096], P(None, 'tensor'), may hold values from -0.0625 to 0.0625
- w_keyval: bfloat16 [8192, 1024], P(None, 'tensor'), may hold values from -0.0625 to 0.0625
- w_out: bfloat16 [4096, 8192], P('tensor'), may hold values from -1 to 1
- kv_cache: bfloat16 [8, 64, 2048, 1024], P(('groups', 'dp'), 'tensor'), parts along dimension 0, may hold values from -305 to 305
- cache_length: int32 [512], P(('groups', 'dp')), parts along dimension 0, may hold values from 1 to 2048, as said below
- row_tenant: int32 [512], P(('groups', 'dp')), parts along dimension 0, may hold values from 0 to 799, as said below
- tenant_lists: int32 [8, 4, 8], P('groups'), parts along dimension 0, may hold values from -1 to 199, as said below
- adapter_heads: bfloat16 [800, 32, 4, 2, 512], P('dp', 'tensor'), may hold values from -6 to 6
- adapter_shared: bfloat16 [800, 16384], P('dp', 'tensor'), may hold values from -6 to 6
Outputs:
- attn_branch: bfloat16 [512, 8192], P(('groups', 'dp'), 'tensor'), parts along dimension 0
The draws below stay inside these ranges and needn't reach their ends.
There are 2 independent parts, one for each index of `groups`. The reference program is written for one: setup_inputs(seed, part) draws one part's arguments, and reference() takes and returns one part's arrays. A program takes and returns all parts, laid end to end along the dimension named above; an argument that names none is the same for every part. Nothing has to cross between parts.
Inputs may be any that keep to these rules, and one draw needn't show every extreme that they name: `tenant_lists`: tenant s * 200 + k is the k-th tenant of store shard s. The entries of one list are distinct; its -1 entries stand at its end and it holds one entry or more. In every draw one data group gets 8 tenants from every store shard. `row_tenant`: row n belongs to data group n // 64. Every row's tenant is listed for its group by its store shard, and every listed tenant is the tenant of some row of that group. `cache_length`: some row has 2048 live positions.
All inputs are finite; a program needn't handle non-finite values.
Results may differ from the reference program's by a relative error of at most 0.012.
The reference program's roundings to bfloat16 on the way count: a program that leaves them out, or rounds other values in their place, can miss the bound.
Values may be sent and summed in bfloat16 or wider, within the bound.
A program may use at most 256 MiB of HBM per device.

```python
import math
import jax
import jax.numpy as jnp
from jax import lax

D = 8192
QH = 32
KVH = 4
HD = 128
I1 = 512
J1 = 16
RANK = 4
SLOTS = 8
ROWS_DEV = 64
CACHE_LEN = 2048
TEN_SHARD = 200
ROWS = 256
TENANTS = 800
N_TENSOR = 4
N_DP = 4


def pick_tenants(key):
    key_count, key_full, key_perm, key_extra, key_shuffle = jax.random.split(key, 5)
    counts = jax.random.randint(key_count, (N_DP, N_DP), 1, SLOTS + 1)
    full_group = jax.random.randint(key_full, (), 0, N_DP)
    column = jnp.arange(N_DP)[None, :]
    counts = jnp.where(column == full_group, SLOTS, counts)
    perm_keys = jax.random.split(key_perm, N_DP * N_DP)
    chosen = jax.vmap(lambda sub_key: jax.random.permutation(sub_key, TEN_SHARD)[:SLOTS])(perm_keys)
    chosen = chosen.reshape(N_DP, N_DP, SLOTS)
    filled = jnp.arange(SLOTS)[None, None, :] < counts[:, :, None]
    lists = jnp.where(filled, chosen, -1).astype(jnp.int32)
    tenant_ids = (jnp.arange(N_DP) * TEN_SHARD)[:, None, None] + chosen
    extra_keys = jax.random.split(key_extra, N_DP)
    shuffle_keys = jax.random.split(key_shuffle, N_DP)

    def group_rows(group, extra_key, shuffle_key):
        group_filled = filled[:, group, :].reshape(-1)
        group_ids = tenant_ids[:, group, :].reshape(-1)
        ordering = jnp.argsort(jnp.where(group_filled, 0, 1), stable=True)
        filled_count = jnp.sum(group_filled.astype(jnp.int32))
        extra = jax.random.randint(extra_key, (ROWS_DEV,), 0, filled_count)
        position = jnp.arange(ROWS_DEV)
        first_pass = ordering[jnp.minimum(position, N_DP * SLOTS - 1)]
        slot_index = jnp.where(position < filled_count, first_pass, ordering[extra])
        return jax.random.permutation(shuffle_key, group_ids[slot_index])
    rows_all = jax.vmap(group_rows)(jnp.arange(N_DP), extra_keys, shuffle_keys)
    return (rows_all.reshape(-1).astype(jnp.int32), lists)


def draw_row_tenant(key, part):
    tenants, lists = pick_tenants(key)
    return tenants


def draw_tenant_lists(key, part):
    tenants, lists = pick_tenants(key)
    return lists


def draw_cache_length(key, part):
    key = jax.random.fold_in(key, 7)
    key_len, key_top = jax.random.split(key, 2)
    lengths = jax.random.randint(key_len, (ROWS,), 1, CACHE_LEN + 1)
    longest = jax.random.randint(key_top, (), 0, ROWS)
    return jnp.where(jnp.arange(ROWS) == longest, CACHE_LEN, lengths).astype(jnp.int32)


def draw_kv_cache(key, part):
    key = jax.random.fold_in(key, 9)
    key_base = jax.random.fold_in(key, 0)
    width = KVH * 2 * HD
    shape = (ROWS, CACHE_LEN, width)
    base = jax.random.truncated_normal(key_base, -6.0, 6.0, shape)
    return base.reshape(N_DP, ROWS_DEV, CACHE_LEN, width).astype(jnp.bfloat16)


def with_spikes(values, own_key, source, target, blocks, factor):
    def block_of(dim):
        return (jnp.arange(values.shape[dim]) // (values.shape[dim] // blocks)).reshape((-1,) + (1,) * (values.ndim - 1 - dim))

    one_side = jax.random.permutation(own_key, blocks)[block_of(target)]
    second = (block_of(target) + blocks // 2) % blocks
    return jnp.where((block_of(source) == one_side) | (block_of(source) == second), factor * values, values)


def shard_levels(rng, shape, cuts, low, largest):
    level, own = 1.0, jax.random.fold_in(rng, 6)
    for dim, shards_of in cuts:
        steps = jnp.exp(jax.random.uniform(jax.random.fold_in(own, dim), (shards_of,), jnp.float32, low / len(cuts), largest / len(cuts)))
        level = level * jnp.repeat(steps, shape[dim] // shards_of).reshape([-1 if axis == dim else 1 for axis in range(len(shape))])
    return level


def noise(own_key, shape, deviation, reach, shards=(), kind=jnp.bfloat16):
    factor_of = shard_levels(own_key, shape, shards, -0.22, 0.18) if shards else 1.0
    drawn = jax.random.normal(own_key, shape, jnp.float32) * deviation * factor_of
    return jnp.minimum(jnp.maximum(drawn, -reach), reach).astype(kind)


def heavy_noise(own_key, extent, deviation, limit, pieces, heavy, kind=jnp.bfloat16):
    drawn = deviation * jax.random.normal(own_key, extent, jnp.float32)
    if pieces:
        drawn = drawn * shard_levels(own_key, extent, pieces, -0.22, 0.18)
    return jnp.clip(with_spikes(drawn, jax.random.fold_in(own_key, 3), *heavy), -limit, limit).astype(kind)


def setup_inputs(seed: int = 0, part: int = 0) -> dict:
    streams_of = jax.random.split(jax.random.key(seed), 12)
    own_keys = jax.random.split(jax.random.fold_in(streams_of[11], part), 12)
    return {
        "hidden_in": noise(own_keys[0], (ROWS, D), 1.0, 6.0, ((0, 4), (1, 4))),
        "norm_gain": jnp.clip(1.0 + 0.18 * jax.random.normal(streams_of[1], (D,), jnp.float32), 0.099609375, 1.8984375).astype(jnp.bfloat16),
        "w_query": noise(streams_of[2], (D, QH * HD), D ** -0.5, 0.0625, ((1, 4),)),
        "w_keyval": noise(streams_of[3], (D, KVH * 2 * HD), D ** -0.5, 0.0625, ((1, 4),)),
        "w_out": heavy_noise(streams_of[4], (QH * HD, D), 64 ** -0.5, 1.0, ((0, 4),), (0, 1, 4, 2.0)),
        "kv_cache": draw_kv_cache(jax.random.fold_in(jax.random.fold_in(streams_of[11], part), 71), part),
        "cache_length": draw_cache_length(jax.random.fold_in(jax.random.fold_in(streams_of[11], part), 71), part),
        "row_tenant": draw_row_tenant(jax.random.fold_in(jax.random.fold_in(streams_of[11], part), 71), part),
        "tenant_lists": draw_tenant_lists(jax.random.fold_in(jax.random.fold_in(streams_of[11], part), 71), part),
        "adapter_heads": noise(streams_of[9], (TENANTS, QH, RANK, 2, I1), 1.0, 6.0, ((0, 4), (1, 4))),
        "adapter_shared": noise(streams_of[10], (TENANTS, 2 * RANK * J1 * HD), 1.0, 6.0, ((0, 4), (1, 4))),
    }


FLOOR_SCORE = -1e+30
OUT_SCALE = 8.0

def rounded(values):
    return lax.optimization_barrier(values.astype(jnp.bfloat16))

def reference(hidden_in, norm_gain, w_query, w_keyval, w_out, kv_cache, cache_length, row_tenant, tenant_lists, adapter_heads, adapter_shared):
    row_count = hidden_in.shape[0]
    group_size = QH // KVH
    widened = hidden_in.astype(jnp.float32)
    inverse = lax.rsqrt(lax.optimization_barrier(jnp.mean(widened * widened, axis=1, keepdims=True)) + 1e-05)
    normed = (widened * inverse * norm_gain.astype(jnp.float32)).astype(jnp.bfloat16)
    group = jnp.arange(row_count, dtype=jnp.int32) // ROWS_DEV
    shard = row_tenant // TEN_SHARD
    within = row_tenant - shard * TEN_SHARD
    wanted = tenant_lists[shard, group]
    listed = jnp.any(wanted == within[:, None], axis=1).astype(jnp.bfloat16)
    factor_heads = adapter_heads[row_tenant] * listed[:, None, None, None, None]
    factor_shared = adapter_shared[row_tenant] * listed[:, None]
    blocks = normed.reshape(row_count, I1, J1)
    inner = rounded(jnp.einsum('nhri,nij->nhrj', factor_heads[:, :, :, 0, :].astype(jnp.float32), blocks.astype(jnp.float32)))
    query_factor = factor_shared[:, :RANK * J1 * HD].reshape(row_count, RANK, J1, HD)
    query_delta = jnp.einsum('nhrj,nrje->nhe', inner.astype(jnp.float32), query_factor.astype(jnp.float32)).reshape(row_count, QH * HD)
    query = rounded(jnp.dot(normed, w_query, preferred_element_type=jnp.float32) + 1.0 / math.sqrt(RANK * D) * query_delta)
    keyval = rounded(jnp.dot(normed, w_keyval, preferred_element_type=jnp.float32))
    score_coeff = 1.0 / math.sqrt(HD)
    cache_rows = kv_cache.reshape(row_count, CACHE_LEN, KVH * 2 * HD)

    def attend(items):
        query_row, keyval_row, cache_row, length = items
        grouped = query_row.astype(jnp.float32).reshape(KVH, group_size, HD)
        grid = cache_row.astype(jnp.float32).reshape(CACHE_LEN, KVH, 2, HD)
        newest = keyval_row.astype(jnp.float32).reshape(KVH, 2, HD)
        scores = jnp.einsum('kgd,pkd->kgp', grouped, grid[:, :, 0, :]) * score_coeff
        visible = jnp.arange(CACHE_LEN, dtype=jnp.int32) < length
        scores = jnp.where(visible[None, None, :], scores, FLOOR_SCORE)
        own_score = jnp.einsum('kgd,kd->kg', grouped, newest[:, 0, :]) * score_coeff
        peak = jnp.maximum(lax.optimization_barrier(jnp.max(scores, axis=2)), own_score)
        expo = jnp.exp(scores - peak[:, :, None])
        expo_new = jnp.exp(own_score - peak)
        totals = lax.optimization_barrier(jnp.sum(expo, axis=2)) + expo_new
        weights = rounded(expo).astype(jnp.float32)
        weight_new = rounded(expo_new).astype(jnp.float32)
        summed = jnp.einsum('kgp,pkd->kgd', weights, grid[:, :, 1, :]) + weight_new[:, :, None] * newest[:, None, 1, :]
        return rounded(summed / totals[:, :, None]).reshape(QH * HD)
    attended = lax.map(attend, (query, keyval, cache_rows, cache_length))
    heads_view = attended.astype(jnp.float32).reshape(row_count, QH, HD)
    out_factor = factor_shared[:, RANK * J1 * HD:].reshape(row_count, RANK, HD, J1)
    mixed_factor = rounded(jnp.einsum('nhe,nrej->nrhj', heads_view, out_factor.astype(jnp.float32))).astype(jnp.float32)
    out_heads = factor_heads[:, :, :, 1, :]
    per_block = QH // N_TENSOR
    out_coeff = OUT_SCALE / math.sqrt(RANK * QH * HD)

    def block_sum(total, block):
        first = (block * per_block).astype(jnp.int32)
        head_cols = lax.dynamic_slice_in_dim(attended, first * HD, per_block * HD, 1)
        weight_rows = lax.dynamic_slice_in_dim(w_out, first * HD, per_block * HD, 0)
        base = jnp.dot(head_cols, weight_rows, preferred_element_type=jnp.float32)
        mixed_block = lax.dynamic_slice_in_dim(mixed_factor, first, per_block, 2)
        heads_block = lax.dynamic_slice_in_dim(out_heads, first, per_block, 1).astype(jnp.float32)
        delta = jnp.einsum('nrhj,nhri->nij', mixed_block, heads_block).reshape(row_count, D)
        part = rounded(base + out_coeff * delta).astype(jnp.float32)
        return (total + part, None)
    total, unused = lax.scan(block_sum, jnp.zeros((row_count, D), jnp.float32), jnp.arange(N_TENSOR, dtype=jnp.int32))
    return total.astype(jnp.bfloat16)
```

```python
import functools
import math

import jax
import jax.numpy as jnp
from jax import lax
from jax.experimental import pallas as pl
from jax.experimental.pallas import tpu as pltpu
from jax.sharding import PartitionSpec as P

D = 8192
QH = 32
KVH = 4
HD = 128
I1 = 512
J1 = 16
RANK = 4
FLOOR_SCORE = -1e30
OUT_SCALE = 8.0
GRAIN = 256
F32 = jnp.float32
BF16 = jnp.bfloat16
VMEM_BYTES = 56 * 1024 * 1024


def params(**more):
    return pltpu.CompilerParams(vmem_limit_bytes=VMEM_BYTES, **more)


def nt_dot(left, right):
    return lax.dot_general(left, right, (((1,), (1,)), ((), ())), preferred_element_type=F32)


def pick_kernel(count, index_ref, store_ref, out_ref, sems):
    def start(k, carry):
        pltpu.make_async_copy(store_ref.at[index_ref[k]], out_ref.at[k], sems.at[k]).start()
        return carry

    def finish(k, carry):
        pltpu.make_async_copy(store_ref.at[0], out_ref.at[k], sems.at[k]).wait()
        return carry

    lax.fori_loop(0, count, start, 0)
    lax.fori_loop(0, count, finish, 0)


def pick_tenants(indices, store):
    count = indices.shape[0]
    return pl.pallas_call(
        functools.partial(pick_kernel, count),
        grid_spec=pltpu.PrefetchScalarGridSpec(
            num_scalar_prefetch=1,
            grid=(1,),
            in_specs=[pl.BlockSpec(memory_space=pl.ANY)],
            out_specs=pl.BlockSpec(memory_space=pl.ANY),
            scratch_shapes=[pltpu.SemaphoreType.DMA((count,))],
        ),
        out_shape=jax.ShapeDtypeStruct((count,) + store.shape[1:], store.dtype),
        compiler_params=params(),
    )(indices, store)


def project_kernel(depth, hidden_ref, gain_ref, wq_ref, wkv_ref, normed_ref, base_ref, keyval_ref, acc):
    step = pl.program_id(0)

    @pl.when(step == 0)
    def _():
        wide = hidden_ref[...].astype(F32)
        inverse = lax.rsqrt(jnp.mean(wide * wide, axis=1, keepdims=True) + 1e-05)
        normed_ref[...] = (wide * inverse * gain_ref[...].astype(F32)).astype(BF16)
        base_ref[...] = jnp.zeros_like(base_ref)
        acc[...] = jnp.zeros_like(acc)

    part = normed_ref[:, pl.ds(pl.multiple_of(step * depth, depth), depth)]
    base_ref[...] += jnp.dot(part, wq_ref[...], preferred_element_type=F32)
    acc[...] += jnp.dot(part, wkv_ref[...], preferred_element_type=F32)

    @pl.when(step == pl.num_programs(0) - 1)
    def _():
        keyval_ref[...] = acc[...].astype(BF16)


def project(hidden, gain, w_query, w_keyval):
    rows = hidden.shape[0]
    depth = 1024
    q_cols, kv_cols = w_query.shape[1], w_keyval.shape[1]
    whole = lambda k: (0, 0)
    return pl.pallas_call(
        functools.partial(project_kernel, depth),
        grid=(D // depth,),
        in_specs=[
            pl.BlockSpec((rows, D), whole),
            pl.BlockSpec((1, D), whole),
            pl.BlockSpec((depth, q_cols), lambda k: (k, 0)),
            pl.BlockSpec((depth, kv_cols), lambda k: (k, 0)),
        ],
        out_specs=[
            pl.BlockSpec((rows, D), whole),
            pl.BlockSpec((rows, q_cols), whole),
            pl.BlockSpec((rows, kv_cols), whole),
        ],
        out_shape=[
            jax.ShapeDtypeStruct((rows, D), BF16),
            jax.ShapeDtypeStruct((rows, q_cols), F32),
            jax.ShapeDtypeStruct((rows, kv_cols), BF16),
        ],
        scratch_shapes=[pltpu.VMEM((rows, kv_cols), F32)],
        compiler_params=params(),
        cost_estimate=pl.CostEstimate(
            flops=2 * rows * D * (q_cols + kv_cols),
            bytes_accessed=2 * D * (q_cols + kv_cols),
            transcendentals=0,
        ),
    )(hidden, gain.reshape(1, D), w_query, w_keyval)


def query_kernel(heads, normed_ref, factor_ref, shared_ref, mask_ref, base_ref, query_ref, turned, spread, inner):
    rows = normed_ref.shape[0]
    lanes = mask_ref.shape[1]
    half = D // 2
    piece = half // 4
    for c in range(4):
        both = jnp.concatenate(
            [normed_ref[:, c * piece : (c + 1) * piece], normed_ref[:, half + c * piece : half + (c + 1) * piece]],
            axis=0,
        ).astype(F32)
        turned[c * piece : (c + 1) * piece, :] = both.T
    for j in range(J1):
        back = turned[pl.ds(j, I1 // 2, stride=J1), :].T
        spread[j * rows : (j + 1) * rows, : I1 // 2] = back[:rows].astype(BF16)
        spread[j * rows : (j + 1) * rows, I1 // 2 :] = back[rows:].astype(BF16)
    mask = mask_ref[...]
    for h in range(heads):
        factor = jnp.concatenate([factor_ref[s, h] for s in range(factor_ref.shape[0])], axis=0)
        for j0 in range(0, J1, 4):
            part = nt_dot(spread[j0 * rows : (j0 + 4) * rows, :], factor)
            for j in range(4):
                own = jnp.where(mask > 0, part[j * rows : (j + 1) * rows], 0.0)
                inner[j0 + j, h * rows : (h + 1) * rows, :] = own.astype(BF16)
    delta = jnp.zeros((heads * rows, HD), F32)
    for j in range(J1):
        delta += jnp.dot(inner[j], shared_ref[:, j * HD : (j + 1) * HD], preferred_element_type=F32)
    coeff = 1.0 / math.sqrt(RANK * D)
    for h in range(heads):
        cols = slice(h * HD, (h + 1) * HD)
        query_ref[:, cols] = (base_ref[:, cols] + coeff * delta[h * rows : (h + 1) * rows]).astype(BF16)


def adapt_query(normed, factors, shared, mask, base):
    rows, cols = base.shape
    heads = cols // HD
    return pl.pallas_call(
        functools.partial(query_kernel, heads),
        out_shape=jax.ShapeDtypeStruct((rows, cols), BF16),
        scratch_shapes=[
            pltpu.VMEM((D // 2, 2 * rows), F32),
            pltpu.VMEM((J1 * rows, I1), BF16),
            pltpu.VMEM((J1, heads * rows, mask.shape[1]), BF16),
        ],
        compiler_params=params(),
    )(normed, factors, shared, mask, base)


def attend_kernel(slots, length_ref, query_ref, fresh_ref, cache_ref, out_ref, held, scores, sems):
    rows, span = cache_ref.shape[0], cache_ref.shape[1]
    per_group = QH // KVH
    pieces = span // GRAIN
    coeff = 1.0 / math.sqrt(HD)

    def chunks_of(row):
        return (length_ref[row] + (GRAIN - 1)) // GRAIN

    def copy_of(row, c):
        slot = lax.rem(row, slots)
        where = pl.ds(pl.multiple_of(c * GRAIN, GRAIN), GRAIN)
        return pltpu.make_async_copy(
            cache_ref.at[row, where], held.at[slot, where], sems.at[slot, c]
        )

    def fetch(row):
        def one(c, carry):
            copy_of(row, c).start()
            return carry

        lax.fori_loop(0, chunks_of(row), one, 0)

    for row in range(min(slots - 1, rows)):
        fetch(row)

    def per_row(row, carry):
        @pl.when(row + slots - 1 < rows)
        def _():
            fetch(row + slots - 1)

        slot = lax.rem(row, slots)
        count = chunks_of(row)
        length = length_ref[row]
        query = query_ref[row]
        newest = fresh_ref[row].astype(F32)
        own_parts, value_parts = [], []
        for g in range(KVH):
            heads = slice(g * per_group, (g + 1) * per_group)
            key = newest[2 * g : 2 * g + 1]
            own_parts.append(jnp.sum(query[heads].astype(F32) * key, axis=1, keepdims=True))
            value_parts.append(jnp.broadcast_to(newest[2 * g + 1 : 2 * g + 2], (per_group, HD)))
        own = jnp.concatenate(own_parts, axis=0) * coeff
        value_new = jnp.concatenate(value_parts, axis=0)

        def finish(c, carry):
            copy_of(row, c).wait()
            return carry

        for n in range(1, pieces + 1):
            @pl.when(count == n)
            def _(n=n):
                for c in range(n):
                    finish(c, 0)
                    where = slice(c * GRAIN, (c + 1) * GRAIN)
                    for g in range(KVH):
                        heads = slice(g * per_group, (g + 1) * per_group)
                        keys = held[slot, where, 2 * g * HD : (2 * g + 1) * HD]
                        scores[heads, where] = nt_dot(query[heads], keys) * coeff
                width = n * GRAIN
                full = scores[:, :width]
                spot = lax.broadcasted_iota(jnp.int32, (QH, width), 1)
                full = jnp.where(spot < length, full, FLOOR_SCORE)
                peak = jnp.maximum(jnp.max(full, axis=1, keepdims=True), own)
                expo = jnp.exp(full - peak)
                expo_new = jnp.exp(own - peak)
                total = jnp.sum(expo, axis=1, keepdims=True) + expo_new
                weight = expo.astype(BF16)
                weight_new = expo_new.astype(BF16).astype(F32)
                summed = jnp.concatenate(
                    [
                        jnp.dot(
                            weight[g * per_group : (g + 1) * per_group],
                            held[slot, :width, (2 * g + 1) * HD : (2 * g + 2) * HD],
                            preferred_element_type=F32,
                        )
                        for g in range(KVH)
                    ],
                    axis=0,
                )
                out_ref[row] = ((summed + weight_new * value_new) / total).astype(BF16)

        return carry

    lax.fori_loop(0, rows, per_row, 0)


def attend(lengths, queries, fresh, cache):
    rows, span, width = cache.shape
    slots = min(4, rows + 1)
    return pl.pallas_call(
        functools.partial(attend_kernel, slots),
        in_specs=[
            pl.BlockSpec(memory_space=pltpu.SMEM),
            pl.BlockSpec(memory_space=pltpu.VMEM),
            pl.BlockSpec(memory_space=pltpu.VMEM),
            pl.BlockSpec(memory_space=pl.ANY),
        ],
        out_specs=pl.BlockSpec(memory_space=pltpu.VMEM),
        out_shape=jax.ShapeDtypeStruct((rows, QH, HD), BF16),
        scratch_shapes=[
            pltpu.VMEM((slots, span, width), BF16),
            pltpu.VMEM((QH, span), F32),
            pltpu.SemaphoreType.DMA((slots, span // GRAIN)),
        ],
        compiler_params=params(),
        cost_estimate=pl.CostEstimate(
            flops=4 * rows * span * QH * HD,
            bytes_accessed=rows * span * width,
            transcendentals=rows * span * QH,
        ),
    )(lengths, queries, fresh, cache)


def output_kernel(heads, att_ref, factor_ref, shared_ref, mask_ref, low_ref, high_ref, out_ref, turned, mixed, factors, spread):
    step = pl.program_id(0)
    rows = att_ref.shape[0]
    lanes = mask_ref.shape[1]
    width = low_ref.shape[1]
    half = I1 // 2

    @pl.when(step == 0)
    def _():
        for c in range(4):
            cols = slice(c * I1, (c + 1) * I1)
            turned[cols, :] = shared_ref[:, cols].astype(F32).T
        stack = jnp.concatenate([att_ref[:, h * HD : (h + 1) * HD] for h in range(heads)], axis=0)
        mask = mask_ref[...]
        for j in range(J1):
            table = turned[pl.ds(j, HD, stride=J1), :].astype(BF16)
            part = jnp.dot(stack, table, preferred_element_type=F32)
            for h in range(heads):
                own = jnp.where(mask > 0, part[h * rows : (h + 1) * rows], 0.0)
                mixed[j * rows : (j + 1) * rows, h * lanes : (h + 1) * lanes] = own.astype(BF16)
        sources = factor_ref.shape[0]
        depth = factor_ref.shape[2]
        for h in range(heads):
            for s in range(sources):
                first = h * lanes + s * depth
                factors[first : first + depth, :] = factor_ref[s, h]
        for j0 in range(0, J1, 4):
            delta = jnp.dot(mixed[j0 * rows : (j0 + 4) * rows, :], factors[...], preferred_element_type=F32)
            for j in range(4):
                own = delta[j * rows : (j + 1) * rows]
                both = jnp.concatenate([own[:, :half], own[:, half:]], axis=0)
                spread[pl.ds(j0 + j, half, stride=J1), :] = both.T

    coeff = OUT_SCALE / math.sqrt(RANK * QH * HD)
    delta = spread[pl.ds(pl.multiple_of(step * width, width), width), :].T
    att = att_ref[...]
    for side, weight in enumerate((low_ref, high_ref)):
        base = jnp.dot(att, weight[...], preferred_element_type=F32)
        out_ref[side] = (base + coeff * delta[side * rows : (side + 1) * rows]).astype(BF16)


def project_out(attended, factors, shared, mask, w_out):
    rows, inner = attended.shape
    heads = inner // HD
    lanes = mask.shape[1]
    width = 512
    steps = D // 2 // width
    whole2 = lambda k: (0, 0)
    out = pl.pallas_call(
        functools.partial(output_kernel, heads),
        grid=(steps,),
        in_specs=[
            pl.BlockSpec((rows, inner), whole2),
            pl.BlockSpec(factors.shape, lambda k: (0, 0, 0, 0)),
            pl.BlockSpec(shared.shape, whole2),
            pl.BlockSpec(mask.shape, whole2),
            pl.BlockSpec((inner, width), lambda k: (0, k)),
            pl.BlockSpec((inner, width), lambda k: (0, k + steps)),
        ],
        out_specs=pl.BlockSpec((2, rows, width), lambda k: (0, 0, k)),
        out_shape=jax.ShapeDtypeStruct((2, rows, D // 2), BF16),
        scratch_shapes=[
            pltpu.VMEM((J1 * HD, lanes), F32),
            pltpu.VMEM((J1 * rows, heads * lanes), BF16),
            pltpu.VMEM((heads * lanes, I1), BF16),
            pltpu.VMEM((D // 2, 2 * rows), F32),
        ],
        compiler_params=params(),
    )(attended, factors, shared, mask, w_out, w_out)
    return out


def on_device(
    hidden_in,
    norm_gain,
    w_query,
    w_keyval,
    w_out,
    kv_cache,
    cache_length,
    row_tenant,
    tenant_lists,
    adapter_heads,
    adapter_shared,
):
    groups, slots = tenant_lists.shape[0], tenant_lists.shape[2]
    stored, heads_here = adapter_heads.shape[:2]
    dp = lax.axis_index("dp")
    outgoing = lax.dynamic_index_in_dim(tenant_lists, dp, 0, keepdims=False).reshape(-1)

    hidden = lax.all_gather(hidden_in, "tensor", axis=1, tiled=True)
    picker = (outgoing[:, None] == jnp.arange(stored, dtype=jnp.int32)[None, :]).astype(BF16)
    send_shared = (
        jnp.dot(picker, adapter_shared, preferred_element_type=F32)
        .astype(BF16)
        .reshape(groups, slots, adapter_shared.shape[1])
    )
    got_shared = lax.all_to_all(send_shared, "dp", split_axis=0, concat_axis=0, tiled=True)
    everyone = lax.all_gather(got_shared, "tensor", axis=2, tiled=True)
    tables = everyone.reshape(groups * slots, 2, RANK, J1 * HD)
    lanes = groups * slots * RANK
    shared_query = tables[:, 0].reshape(lanes, J1 * HD)
    shared_out = tables[:, 1].reshape(lanes, J1 * HD)

    picked = pick_tenants(jnp.maximum(outgoing, 0), adapter_heads)
    picked = picked.reshape(groups, slots, heads_here, RANK, 2, I1)

    def exchange(part):
        send = picked[:, :, :, :, part, :].transpose(0, 2, 1, 3, 4)
        send = send.reshape(groups, heads_here, slots * RANK, I1)
        return lax.all_to_all(send, "dp", split_axis=0, concat_axis=0, tiled=True)

    heads_query = exchange(0)
    heads_out = exchange(1)

    incoming = lax.dynamic_index_in_dim(tenant_lists, dp, 1, keepdims=False)
    ids = jnp.where(incoming >= 0, jnp.arange(groups, dtype=jnp.int32)[:, None] * stored + incoming, -1)
    ids = jnp.repeat(ids.reshape(-1), RANK)
    mask = (row_tenant[:, None] == ids[None, :]).astype(F32)

    normed, base, keyval = project(hidden, norm_gain, w_query, w_keyval)
    query = adapt_query(normed, heads_query, shared_query, mask, base)

    rows_here, span, width = kv_cache.shape[1:]
    both = jnp.concatenate([query, keyval], axis=1)
    both = lax.all_to_all(both, "tensor", split_axis=0, concat_axis=0, tiled=True)
    parts = both.reshape(-1, rows_here, both.shape[1])
    q_cols = query.shape[1]
    queries = parts[:, :, :q_cols].transpose(1, 0, 2).reshape(rows_here, QH, HD)
    fresh = parts[:, :, q_cols:].transpose(1, 0, 2).reshape(rows_here, 2 * KVH, HD)
    first_row = lax.axis_index("tensor") * rows_here
    lengths = lax.dynamic_slice_in_dim(cache_length, first_row, rows_here, 0)
    attended = attend(lengths, queries, fresh, kv_cache.reshape(rows_here, span, width))
    attended = lax.all_to_all(
        attended.reshape(rows_here, QH * HD), "tensor", split_axis=1, concat_axis=0, tiled=True
    )
    partial = project_out(attended, heads_out, shared_out, mask, w_out)
    row_count = partial.shape[1]
    partial = partial.transpose(1, 0, 2).reshape(row_count, D)
    return lax.psum_scatter(partial, "tensor", scatter_dimension=1, tiled=True)


def solution(mesh):
    placed = (
        P(("groups", "dp"), "tensor"),
        P(),
        P(None, "tensor"),
        P(None, "tensor"),
        P("tensor", None),
        P(("groups", "dp"), "tensor", None, None),
        P(("groups", "dp")),
        P(("groups", "dp")),
        P("groups", None, None),
        P("dp", "tensor", None, None, None),
        P("dp", "tensor"),
    )
    return jax.shard_map(
        on_device,
        mesh=mesh,
        in_specs=placed,
        out_specs=P(("groups", "dp"), "tensor"),
        check_vma=False,
    )
```

```python
import functools
import math

import jax
import jax.numpy as jnp
from jax import lax
from jax.experimental import pallas as pl
from jax.experimental.pallas import tpu as pltpu
from jax.sharding import PartitionSpec as P

D = 8192
QH = 32
KVH = 4
HD = 128
I1 = 512
J1 = 16
RANK = 4
FLOOR_SCORE = -1e30
OUT_SCALE = 8.0
GRAIN = 256
F32 = jnp.float32
BF16 = jnp.bfloat16
VMEM_BYTES = 56 * 1024 * 1024


def params(**more):
    return pltpu.CompilerParams(vmem_limit_bytes=VMEM_BYTES, **more)


def nt_dot(left, right):
    return lax.dot_general(left, right, (((1,), (1,)), ((), ())), preferred_element_type=F32)


def pick_kernel(count, index_ref, store_ref, out_ref, sems):
    for k in range(count):
        pltpu.make_async_copy(store_ref.at[index_ref[k]], out_ref.at[k], sems.at[k]).start()
    for k in range(count):
        pltpu.make_async_copy(store_ref.at[index_ref[k]], out_ref.at[k], sems.at[k]).wait()


def pick_tenants(indices, store):
    count = indices.shape[0]
    return pl.pallas_call(
        functools.partial(pick_kernel, count),
        in_specs=[
            pl.BlockSpec(memory_space=pltpu.SMEM),
            pl.BlockSpec(memory_space=pl.ANY),
        ],
        out_specs=pl.BlockSpec(memory_space=pltpu.VMEM),
        scratch_shapes=[pltpu.SemaphoreType.DMA((count,))],
        out_shape=jax.ShapeDtypeStruct((count,) + store.shape[1:], store.dtype),
        compiler_params=params(),
    )(indices, store)


def project_kernel(depth, hidden_ref, gain_ref, wq_ref, wkv_ref, normed_ref, base_ref, keyval_ref, acc):
    step = pl.program_id(0)

    @pl.when(step == 0)
    def _():
        wide = hidden_ref[...].astype(F32)
        inverse = lax.rsqrt(jnp.mean(wide * wide, axis=1, keepdims=True) + 1e-05)
        normed_ref[...] = (wide * inverse * gain_ref[...].astype(F32)).astype(BF16)
        base_ref[...] = jnp.zeros_like(base_ref)
        acc[...] = jnp.zeros_like(acc)

    part = normed_ref[:, pl.ds(pl.multiple_of(step * depth, depth), depth)]
    base_ref[...] += jnp.dot(part, wq_ref[...], preferred_element_type=F32)
    acc[...] += jnp.dot(part, wkv_ref[...], preferred_element_type=F32)

    @pl.when(step == pl.num_programs(0) - 1)
    def _():
        keyval_ref[...] = acc[...].astype(BF16)


def project(hidden, gain, w_query, w_keyval):
    rows = hidden.shape[0]
    depth = 1024
    q_cols, kv_cols = w_query.shape[1], w_keyval.shape[1]
    whole = lambda k: (0, 0)
    return pl.pallas_call(
        functools.partial(project_kernel, depth),
        grid=(D // depth,),
        in_specs=[
            pl.BlockSpec((rows, D), whole),
            pl.BlockSpec((1, D), whole),
            pl.BlockSpec((depth, q_cols), lambda k: (k, 0)),
            pl.BlockSpec((depth, kv_cols), lambda k: (k, 0)),
        ],
        out_specs=[
            pl.BlockSpec((rows, D), whole),
            pl.BlockSpec((rows, q_cols), whole),
            pl.BlockSpec((rows, kv_cols), whole),
        ],
        out_shape=[
            jax.ShapeDtypeStruct((rows, D), BF16),
            jax.ShapeDtypeStruct((rows, q_cols), F32),
            jax.ShapeDtypeStruct((rows, kv_cols), BF16),
        ],
        scratch_shapes=[pltpu.VMEM((rows, kv_cols), F32)],
        compiler_params=params(),
        cost_estimate=pl.CostEstimate(
            flops=2 * rows * D * (q_cols + kv_cols),
            bytes_accessed=2 * D * (q_cols + kv_cols),
            transcendentals=0,
        ),
    )(hidden, gain.reshape(1, D), w_query, w_keyval)


def query_kernel(heads, normed_ref, factor_ref, shared_ref, mask_ref, base_ref, query_ref, turned, spread, inner):
    rows = normed_ref.shape[0]
    lanes = mask_ref.shape[1]
    half = D // 2
    piece = half // 4
    for c in range(4):
        both = jnp.concatenate(
            [normed_ref[:, c * piece : (c + 1) * piece], normed_ref[:, half + c * piece : half + (c + 1) * piece]],
            axis=0,
        ).astype(F32)
        turned[c * piece : (c + 1) * piece, :] = both.T
    for j in range(J1):
        back = turned[pl.ds(j, I1 // 2, stride=J1), :].T
        spread[j * rows : (j + 1) * rows, : I1 // 2] = back[:rows].astype(BF16)
        spread[j * rows : (j + 1) * rows, I1 // 2 :] = back[rows:].astype(BF16)
    mask = mask_ref[...]
    for h in range(heads):
        factor = jnp.concatenate([factor_ref[s, h] for s in range(factor_ref.shape[0])], axis=0)
        for j0 in range(0, J1, 4):
            part = nt_dot(spread[j0 * rows : (j0 + 4) * rows, :], factor)
            for j in range(4):
                own = jnp.where(mask > 0, part[j * rows : (j + 1) * rows], 0.0)
                inner[j0 + j, h * rows : (h + 1) * rows, :] = own.astype(BF16)
    delta = jnp.zeros((heads * rows, HD), F32)
    for j in range(J1):
        delta += jnp.dot(inner[j], shared_ref[:, j * HD : (j + 1) * HD], preferred_element_type=F32)
    coeff = 1.0 / math.sqrt(RANK * D)
    for h in range(heads):
        cols = slice(h * HD, (h + 1) * HD)
        query_ref[:, cols] = (base_ref[:, cols] + coeff * delta[h * rows : (h + 1) * rows]).astype(BF16)


def adapt_query(normed, factors, shared, mask, base):
    rows, cols = base.shape
    heads = cols // HD
    return pl.pallas_call(
        functools.partial(query_kernel, heads),
        out_shape=jax.ShapeDtypeStruct((rows, cols), BF16),
        scratch_shapes=[
            pltpu.VMEM((D // 2, 2 * rows), F32),
            pltpu.VMEM((J1 * rows, I1), BF16),
            pltpu.VMEM((J1, heads * rows, mask.shape[1]), BF16),
        ],
        compiler_params=params(),
    )(normed, factors, shared, mask, base)


def attend_kernel(slots, length_ref, query_ref, fresh_ref, cache_ref, out_ref, held, scores, sems):
    rows, span = cache_ref.shape[0], cache_ref.shape[1]
    per_group = QH // KVH
    pieces = span // GRAIN
    coeff = 1.0 / math.sqrt(HD)

    def chunks_of(row):
        return (length_ref[row] + (GRAIN - 1)) // GRAIN

    def copy_of(row, c):
        slot = lax.rem(row, slots)
        where = pl.ds(pl.multiple_of(c * GRAIN, GRAIN), GRAIN)
        return pltpu.make_async_copy(
            cache_ref.at[row, where], held.at[slot, where], sems.at[slot, c]
        )

    def fetch(row):
        def one(c, carry):
            copy_of(row, c).start()
            return carry

        lax.fori_loop(0, chunks_of(row), one, 0)

    for row in range(min(slots - 1, rows)):
        fetch(row)

    def per_row(row, carry):
        @pl.when(row + slots - 1 < rows)
        def _():
            fetch(row + slots - 1)

        slot = lax.rem(row, slots)
        count = chunks_of(row)
        length = length_ref[row]
        query = query_ref[row]
        newest = fresh_ref[row].astype(F32)
        own_parts, value_parts = [], []
        for g in range(KVH):
            heads = slice(g * per_group, (g + 1) * per_group)
            key = newest[2 * g : 2 * g + 1]
            own_parts.append(jnp.sum(query[heads].astype(F32) * key, axis=1, keepdims=True))
            value_parts.append(jnp.broadcast_to(newest[2 * g + 1 : 2 * g + 2], (per_group, HD)))
        own = jnp.concatenate(own_parts, axis=0) * coeff
        value_new = jnp.concatenate(value_parts, axis=0)

        def finish(c, carry):
            copy_of(row, c).wait()
            return carry

        for n in range(1, pieces + 1):
            @pl.when(count == n)
            def _(n=n):
                for c in range(n):
                    finish(c, 0)
                    where = slice(c * GRAIN, (c + 1) * GRAIN)
                    for g in range(KVH):
                        heads = slice(g * per_group, (g + 1) * per_group)
                        keys = held[slot, where, 2 * g * HD : (2 * g + 1) * HD]
                        scores[heads, where] = nt_dot(query[heads], keys) * coeff
                width = n * GRAIN
                full = scores[:, :width]
                spot = lax.broadcasted_iota(jnp.int32, (QH, width), 1)
                full = jnp.where(spot < length, full, FLOOR_SCORE)
                peak = jnp.maximum(jnp.max(full, axis=1, keepdims=True), own)
                expo = jnp.exp(full - peak)
                expo_new = jnp.exp(own - peak)
                total = jnp.sum(expo, axis=1, keepdims=True) + expo_new
                weight = expo.astype(BF16)
                weight_new = expo_new.astype(BF16).astype(F32)
                summed = jnp.concatenate(
                    [
                        jnp.dot(
                            weight[g * per_group : (g + 1) * per_group],
                            held[slot, :width, (2 * g + 1) * HD : (2 * g + 2) * HD],
                            preferred_element_type=F32,
                        )
                        for g in range(KVH)
                    ],
                    axis=0,
                )
                out_ref[row] = ((summed + weight_new * value_new) / total).astype(BF16)

        return carry

    lax.fori_loop(0, rows, per_row, 0)


def attend(lengths, queries, fresh, cache):
    rows, span, width = cache.shape
    slots = min(4, rows + 1)
    return pl.pallas_call(
        functools.partial(attend_kernel, slots),
        in_specs=[
            pl.BlockSpec(memory_space=pltpu.SMEM),
            pl.BlockSpec(memory_space=pltpu.VMEM),
            pl.BlockSpec(memory_space=pltpu.VMEM),
            pl.BlockSpec(memory_space=pl.ANY),
        ],
        out_specs=pl.BlockSpec(memory_space=pltpu.VMEM),
        out_shape=jax.ShapeDtypeStruct((rows, QH, HD), BF16),
        scratch_shapes=[
            pltpu.VMEM((slots, span, width), BF16),
            pltpu.VMEM((QH, span), F32),
            pltpu.SemaphoreType.DMA((slots, span // GRAIN)),
        ],
        compiler_params=params(),
        cost_estimate=pl.CostEstimate(
            flops=4 * rows * span * QH * HD,
            bytes_accessed=rows * span * width,
            transcendentals=rows * span * QH,
        ),
    )(lengths, queries, fresh, cache)


def output_kernel(
    devices,
    att_ref,
    factor_ref,
    shared_ref,
    mask_ref,
    weight_ref,
    out_ref,
    weights,
    got_att,
    flat_att,
    turned,
    mixed,
    factors,
    spread,
    delta_rows,
    leaving,
    arriving,
    weight_sems,
    att_send,
    att_recv,
    sum_send,
    sum_recv,
):
    me = lax.axis_index("tensor")
    heads, rows_here = att_ref.shape[1], att_ref.shape[2]
    rows, lanes = mask_ref.shape
    width = weights.shape[2]
    half = I1 // 2

    def other(k):
        return lax.rem(me + k, devices)

    def weight_copy(k):
        where = pl.ds(pl.multiple_of(other(k) * width, width), width)
        return pltpu.make_async_copy(weight_ref.at[:, where], weights.at[k], weight_sems.at[k])

    def att_copy(k):
        return pltpu.make_async_remote_copy(
            src_ref=att_ref.at[other(k)],
            dst_ref=got_att.at[me],
            send_sem=att_send.at[k],
            recv_sem=att_recv.at[me],
            device_id={"tensor": other(k)},
            device_id_type=pl.DeviceIdType.MESH,
        )

    def att_arrival(k):
        return pltpu.make_async_remote_copy(
            src_ref=att_ref.at[other(k)],
            dst_ref=got_att.at[other(k)],
            send_sem=att_send.at[k],
            recv_sem=att_recv.at[other(k)],
            device_id={"tensor": other(k)},
            device_id_type=pl.DeviceIdType.MESH,
        )

    def sum_copy(k):
        return pltpu.make_async_remote_copy(
            src_ref=leaving.at[k],
            dst_ref=arriving.at[me],
            send_sem=sum_send.at[k],
            recv_sem=sum_recv.at[me],
            device_id={"tensor": other(k)},
            device_id_type=pl.DeviceIdType.MESH,
        )

    def sum_arrival(k):
        return pltpu.make_async_remote_copy(
            src_ref=leaving.at[k],
            dst_ref=arriving.at[other(k)],
            send_sem=sum_send.at[k],
            recv_sem=sum_recv.at[other(k)],
            device_id={"tensor": other(k)},
            device_id_type=pl.DeviceIdType.MESH,
        )

    barrier = pltpu.get_barrier_semaphore()
    for k in range(1, devices):
        pl.semaphore_signal(
            barrier, inc=1, device_id={"tensor": other(k)}, device_id_type=pl.DeviceIdType.MESH
        )
    order = list(range(1, devices)) + [0]
    for k in order:
        weight_copy(k).start()
    pl.semaphore_wait(barrier, devices - 1)
    for k in range(1, devices):
        att_copy(k).start()

    for c in range(4):
        cols = slice(c * I1, (c + 1) * I1)
        for b in range(lanes // HD):
            turned[b, cols, :] = shared_ref[b * HD : (b + 1) * HD, cols].astype(F32).T
    sources, depth = factor_ref.shape[0], factor_ref.shape[2]
    for h in range(heads):
        for s in range(sources):
            first = h * lanes + s * depth
            factors[first : first + depth, :] = factor_ref[s, h]
    got_att[me] = att_ref[me]
    for k in range(1, devices):
        att_arrival(k).wait_recv()

    stack = [jnp.concatenate([got_att[t, h] for t in range(devices)], axis=0) for h in range(heads)]
    for h in range(heads):
        flat_att[:, h * HD : (h + 1) * HD] = stack[h]
    stack = jnp.concatenate(stack, axis=0)
    mask = mask_ref[...]
    for j in range(J1):
        table = jnp.concatenate(
            [turned[b, pl.ds(j, HD, stride=J1), :] for b in range(lanes // HD)], axis=1
        ).astype(BF16)
        part = jnp.dot(stack, table, preferred_element_type=F32)
        for h in range(heads):
            own = jnp.where(mask > 0, part[h * rows : (h + 1) * rows], 0.0)
            mixed[j * rows : (j + 1) * rows, h * lanes : (h + 1) * lanes] = own.astype(BF16)
    for j0 in range(0, J1, 4):
        delta = jnp.dot(mixed[j0 * rows : (j0 + 4) * rows, :], factors[...], preferred_element_type=F32)
        for j in range(4):
            own = delta[j * rows : (j + 1) * rows]
            both = jnp.concatenate([own[:, :half], own[:, half:]], axis=0)
            spread[pl.ds(j0 + j, half, stride=J1), :] = both.T
    piece = D // 16
    for c in range(8):
        where = slice(c * piece, (c + 1) * piece)
        delta_rows[:, where] = spread[where, :].T

    coeff = OUT_SCALE / math.sqrt(RANK * QH * HD)
    per_half = D // 2 // width

    def partial_of(k):
        weight_copy(k).wait()
        to = other(k)
        first_row = pl.multiple_of((to // per_half) * rows, rows)
        first_col = pl.multiple_of(lax.rem(to, per_half) * width, width)
        base = jnp.dot(flat_att[...], weights[k], preferred_element_type=F32)
        delta = delta_rows[pl.ds(first_row, rows), pl.ds(first_col, width)]
        return (base + coeff * delta).astype(BF16)

    def send_one(k, carry):
        leaving[k] = partial_of(k)
        sum_copy(k).start()
        return carry

    lax.fori_loop(1, devices, send_one, 0)
    total = partial_of(0).astype(F32)
    for k in range(1, devices):
        sum_arrival(k).wait_recv()
        total += arriving[other(k)].astype(F32)
    out_ref[...] = total.astype(BF16)
    for k in range(1, devices):
        att_copy(k).wait_send()
        sum_copy(k).wait_send()


def project_out(attended, factors, shared, mask, w_out):
    devices, heads, rows_here, _ = attended.shape
    rows, lanes = mask.shape
    inner = heads * HD
    width = D // devices
    vmem = pl.BlockSpec(memory_space=pltpu.VMEM)
    return pl.pallas_call(
        functools.partial(output_kernel, devices),
        in_specs=[vmem, vmem, vmem, vmem, pl.BlockSpec(memory_space=pl.ANY)],
        out_specs=vmem,
        out_shape=jax.ShapeDtypeStruct((rows, width), BF16),
        scratch_shapes=[
            pltpu.VMEM((devices, inner, width), BF16),
            pltpu.VMEM((devices, heads, rows_here, HD), BF16),
            pltpu.VMEM((rows, inner), BF16),
            pltpu.VMEM((lanes // HD, J1 * HD, HD), F32),
            pltpu.VMEM((J1 * rows, heads * lanes), BF16),
            pltpu.VMEM((heads * lanes, I1), BF16),
            pltpu.VMEM((D // 2, 2 * rows), F32),
            pltpu.VMEM((2 * rows, D // 2), F32),
            pltpu.VMEM((devices, rows, width), BF16),
            pltpu.VMEM((devices, rows, width), BF16),
            pltpu.SemaphoreType.DMA((devices,)),
            pltpu.SemaphoreType.DMA((devices,)),
            pltpu.SemaphoreType.DMA((devices,)),
            pltpu.SemaphoreType.DMA((devices,)),
            pltpu.SemaphoreType.DMA((devices,)),
        ],
        compiler_params=params(collective_id=1, has_side_effects=True),
    )(attended, factors, shared, mask, w_out)


def on_device(
    hidden_in,
    norm_gain,
    w_query,
    w_keyval,
    w_out,
    kv_cache,
    cache_length,
    row_tenant,
    tenant_lists,
    adapter_heads,
    adapter_shared,
):
    groups, slots = tenant_lists.shape[0], tenant_lists.shape[2]
    stored, heads_here = adapter_heads.shape[:2]
    dp = lax.axis_index("dp")
    outgoing = lax.dynamic_index_in_dim(tenant_lists, dp, 0, keepdims=False).reshape(-1)

    hidden = lax.all_gather(hidden_in, "tensor", axis=1, tiled=True)
    picker = (outgoing[:, None] == jnp.arange(stored, dtype=jnp.int32)[None, :]).astype(BF16)
    send_shared = (
        jnp.dot(picker, adapter_shared, preferred_element_type=F32)
        .astype(BF16)
        .reshape(groups, slots, adapter_shared.shape[1])
    )
    got_shared = lax.all_to_all(send_shared, "dp", split_axis=0, concat_axis=0, tiled=True)
    everyone = lax.all_gather(got_shared, "tensor", axis=2, tiled=True)
    tables = everyone.reshape(groups * slots, 2, RANK, J1 * HD)
    lanes = groups * slots * RANK * 2
    tables = jnp.repeat(tables, 2, axis=2).transpose(1, 0, 2, 3).reshape(2, lanes, J1 * HD)
    shared_query, shared_out = tables[0], tables[1]

    picked = pick_tenants(jnp.maximum(outgoing, 0), adapter_heads)
    picked = picked.reshape(groups, slots, heads_here, RANK * 2, I1).transpose(0, 2, 1, 3, 4)
    picked = picked.reshape(groups, heads_here, slots * RANK * 2, I1)
    factors = lax.all_to_all(picked, "dp", split_axis=0, concat_axis=0, tiled=True)

    incoming = lax.dynamic_index_in_dim(tenant_lists, dp, 1, keepdims=False)
    ids = jnp.where(incoming >= 0, jnp.arange(groups, dtype=jnp.int32)[:, None] * stored + incoming, -1)
    ids = jnp.repeat(ids.reshape(-1), RANK * 2)
    own = row_tenant[:, None] == ids[None, :]
    part = jnp.arange(lanes, dtype=jnp.int32)[None, :] % 2
    mask_query = (own & (part == 0)).astype(F32)
    mask_out = (own & (part == 1)).astype(F32)

    normed, base, keyval = project(hidden, norm_gain, w_query, w_keyval)
    query = adapt_query(normed, factors, shared_query, mask_query, base)

    rows_here, span, width = kv_cache.shape[1:]
    both = jnp.concatenate([query, keyval], axis=1)
    both = lax.all_to_all(both, "tensor", split_axis=0, concat_axis=0, tiled=True)
    parts = both.reshape(-1, rows_here, both.shape[1])
    q_cols = query.shape[1]
    queries = parts[:, :, :q_cols].transpose(1, 0, 2).reshape(rows_here, QH, HD)
    fresh = parts[:, :, q_cols:].transpose(1, 0, 2).reshape(rows_here, 2 * KVH, HD)
    first_row = lax.axis_index("tensor") * rows_here
    lengths = lax.dynamic_slice_in_dim(cache_length, first_row, rows_here, 0)
    attended = attend(lengths, queries, fresh, kv_cache.reshape(rows_here, span, width))
    devices = QH // heads_here
    attended = attended.reshape(rows_here, devices, heads_here, HD).transpose(1, 2, 0, 3)
    return project_out(attended, factors, shared_out, mask_out, w_out)


def solution(mesh):
    placed = (
        P(("groups", "dp"), "tensor"),
        P(),
        P(None, "tensor"),
        P(None, "tensor"),
        P("tensor", None),
        P(("groups", "dp"), "tensor", None, None),
        P(("groups", "dp")),
        P(("groups", "dp")),
        P("groups", None, None),
        P("dp", "tensor", None, None, None),
        P("dp", "tensor"),
    )
    return jax.shard_map(
        on_device,
        mesh=mesh,
        in_specs=placed,
        out_specs=P(("groups", "dp"), "tensor"),
        check_vma=False,
    )
```

```python
import functools
import math

import jax
import jax.numpy as jnp
from jax import lax
from jax.experimental import pallas as pl
from jax.experimental.pallas import tpu as pltpu
from jax.sharding import PartitionSpec as P

D = 8192
QH = 32
KVH = 4
HD = 128
I1 = 512
J1 = 16
RANK = 4
FLOOR_SCORE = -1e30
OUT_SCALE = 8.0
GRAIN = 256
F32 = jnp.float32
BF16 = jnp.bfloat16
VMEM_BYTES = 56 * 1024 * 1024


def params(**more):
    return pltpu.CompilerParams(vmem_limit_bytes=VMEM_BYTES, **more)


def nt_dot(left, right):
    return lax.dot_general(left, right, (((1,), (1,)), ((), ())), preferred_element_type=F32)


def pick_kernel(count, index_ref, store_ref, out_ref, sems):
    for k in range(count):
        pltpu.make_async_copy(store_ref.at[index_ref[k]], out_ref.at[k], sems.at[k]).start()
    for k in range(count):
        pltpu.make_async_copy(store_ref.at[index_ref[k]], out_ref.at[k], sems.at[k]).wait()


def pick_tenants(indices, store):
    count = indices.shape[0]
    return pl.pallas_call(
        functools.partial(pick_kernel, count),
        in_specs=[
            pl.BlockSpec(memory_space=pltpu.SMEM),
            pl.BlockSpec(memory_space=pl.ANY),
        ],
        out_specs=pl.BlockSpec(memory_space=pltpu.VMEM),
        scratch_shapes=[pltpu.SemaphoreType.DMA((count,))],
        out_shape=jax.ShapeDtypeStruct((count,) + store.shape[1:], store.dtype),
        compiler_params=params(),
    )(indices, store)


def mesh_copy(source, target, send_sem, recv_sem, axis, place):
    return pltpu.make_async_remote_copy(
        src_ref=source,
        dst_ref=target,
        send_sem=send_sem,
        recv_sem=recv_sem,
        device_id={axis: place},
        device_id_type=pl.DeviceIdType.MESH,
    )


def expand_shared(blocks, first, lanes, store):
    tenants, width = blocks.shape[1], blocks.shape[2]
    span = J1 * HD
    piece = min(width, span)
    lane = lax.broadcasted_iota(jnp.int32, (lanes, RANK * tenants), 0)
    entry = lax.broadcasted_iota(jnp.int32, (lanes, RANK * tenants), 1)
    wanted = (lane // 2) % RANK * tenants + lane // (2 * RANK)
    chooser = (wanted == entry).astype(F32).astype(BF16)
    for col in range(0, span, piece):
        stack = []
        for r in range(RANK):
            start = first + r * span + col
            local = start % width
            stack.append(blocks[start // width, :, local : local + piece])
        stack = jnp.concatenate(stack, axis=0)
        store(col, piece, jnp.dot(chooser, stack, preferred_element_type=F32))


def front_kernel(
    devices,
    groups,
    hidden_ref,
    gain_ref,
    factor_ref,
    shared_ref,
    mask_ref,
    wq_ref,
    wkv_ref,
    factors_out,
    shared_out,
    rows_out,
    wq,
    wkv,
    hidden,
    factors,
    first_hop,
    blocks,
    normed,
    turned,
    spread,
    inner,
    table,
    leaving,
    arriving,
    weight_sems,
    hidden_send,
    hidden_recv,
    factor_send,
    factor_recv,
    hop_send,
    hop_recv,
    block_send,
    block_recv,
    row_send,
    row_recv,
):
    me, dp = lax.axis_index("tensor"), lax.axis_index("dp")
    rows, lanes = mask_ref.shape
    heads = factor_ref.shape[1]
    width = hidden_ref.shape[1]
    chunks, depth = wq.shape[0], wq.shape[1]
    rows_here = arriving.shape[1]
    q_cols = wq.shape[2]

    def peer(k):
        return lax.rem(me + k, devices)

    def mate(k):
        return lax.rem(dp + k, groups)

    def weight_copies(c):
        where = pl.ds(c * depth, depth)
        return (
            pltpu.make_async_copy(wq_ref.at[where], wq.at[c], weight_sems.at[0, c]),
            pltpu.make_async_copy(wkv_ref.at[where], wkv.at[c], weight_sems.at[1, c]),
        )

    def hidden_copy(k, to):
        return mesh_copy(hidden_ref, hidden.at[to], hidden_send.at[k], hidden_recv.at[to], "tensor", peer(k))

    def block_copy(k, to):
        return mesh_copy(blocks.at[me], blocks.at[to], block_send.at[k], block_recv.at[to], "tensor", peer(k))

    def row_copy(k, to):
        return mesh_copy(leaving.at[peer(k)], arriving.at[to], row_send.at[k], row_recv.at[to], "tensor", peer(k))

    def hop_copy(k, to):
        return mesh_copy(shared_ref.at[mate(k)], first_hop.at[to], hop_send.at[k], hop_recv.at[to], "dp", mate(k))

    def factor_copy(k, to):
        return mesh_copy(factor_ref.at[mate(k)], factors.at[to], factor_send.at[k], factor_recv.at[to], "dp", mate(k))

    barrier = pltpu.get_barrier_semaphore()
    for k in range(1, devices):
        pl.semaphore_signal(barrier, inc=1, device_id={"tensor": peer(k)}, device_id_type=pl.DeviceIdType.MESH)
    for k in range(1, groups):
        pl.semaphore_signal(barrier, inc=1, device_id={"dp": mate(k)}, device_id_type=pl.DeviceIdType.MESH)
    for c in range(chunks):
        for copy in weight_copies(c):
            copy.start()
    pl.semaphore_wait(barrier, devices - 1 + groups - 1)
    for k in range(1, groups):
        hop_copy(k, dp).start()
    for k in range(1, devices):
        hidden_copy(k, me).start()
    for k in range(1, groups):
        factor_copy(k, dp).start()
    first_hop[dp] = shared_ref[dp]
    hidden[me] = hidden_ref[...]
    factors[dp] = factor_ref[dp]
    for k in range(1, groups):
        hop_copy(k, mate(k)).wait_recv()
    blocks[me] = jnp.concatenate([first_hop[s].astype(F32) for s in range(groups)], axis=0).astype(BF16)
    for k in range(1, devices):
        block_copy(k, me).start()

    for k in range(1, devices):
        hidden_copy(k, peer(k)).wait_recv()
    squares = jnp.zeros((rows, 1), F32)
    for t in range(devices):
        wide = hidden[t].astype(F32)
        squares += jnp.sum(wide * wide, axis=1, keepdims=True)
    inverse = lax.rsqrt(squares / D + 1e-05)
    for t in range(devices):
        where = slice(t * width, (t + 1) * width)
        normed[:, where] = (hidden[t].astype(F32) * inverse * gain_ref[:, where].astype(F32)).astype(BF16)
    base = jnp.zeros((rows, q_cols), F32)
    keyval = jnp.zeros((rows, wkv.shape[2]), F32)
    for c in range(chunks):
        for copy in weight_copies(c):
            copy.wait()
        part = normed[:, c * depth : (c + 1) * depth]
        base += jnp.dot(part, wq[c], preferred_element_type=F32)
        keyval += jnp.dot(part, wkv[c], preferred_element_type=F32)

    half = D // 2
    piece = half // 4
    for c in range(4):
        both = jnp.concatenate(
            [normed[:, c * piece : (c + 1) * piece], normed[:, half + c * piece : half + (c + 1) * piece]],
            axis=0,
        ).astype(F32)
        turned[c * piece : (c + 1) * piece, :] = both.T
    for j in range(J1):
        back = turned[pl.ds(j, I1 // 2, stride=J1), :].T
        spread[j * rows : (j + 1) * rows, : I1 // 2] = back[:rows].astype(BF16)
        spread[j * rows : (j + 1) * rows, I1 // 2 :] = back[rows:].astype(BF16)

    for k in range(1, groups):
        factor_copy(k, mate(k)).wait_recv()
    mask = mask_ref[...]
    for h in range(heads):
        factor = jnp.concatenate([factors[s, h] for s in range(groups)], axis=0)
        for j0 in range(0, J1, 4):
            part = nt_dot(spread[j0 * rows : (j0 + 4) * rows, :], factor)
            for j in range(4):
                own = jnp.where(mask > 0, part[j * rows : (j + 1) * rows], 0.0)
                inner[j0 + j, h * rows : (h + 1) * rows, :] = own.astype(BF16)
    factors_out[...] = factors[...]

    for k in range(1, devices):
        block_copy(k, peer(k)).wait_recv()

    def store(col, size, value):
        table[:, col : col + size] = value.astype(BF16)

    expand_shared(blocks, 0, lanes, store)
    shared_out[...] = blocks[...]
    delta = jnp.zeros((heads * rows, HD), F32)
    for j in range(J1):
        delta += jnp.dot(inner[j], table[:, j * HD : (j + 1) * HD], preferred_element_type=F32)
    coeff = 1.0 / math.sqrt(RANK * D)
    query = jnp.concatenate(
        [base[:, h * HD : (h + 1) * HD] + coeff * delta[h * rows : (h + 1) * rows] for h in range(heads)], axis=1
    )
    for t in range(devices):
        where = slice(t * rows_here, (t + 1) * rows_here)
        leaving[t, :, :q_cols] = query[where].astype(BF16)
        leaving[t, :, q_cols:] = keyval[where].astype(BF16)
    for k in range(1, devices):
        row_copy(k, me).start()
    arriving[me] = leaving[me]
    for k in range(1, devices):
        row_copy(k, peer(k)).wait_recv()
    rows_out[...] = arriving[...]
    for k in range(1, devices):
        hidden_copy(k, me).wait_send()
        block_copy(k, me).wait_send()
        row_copy(k, me).wait_send()
    for k in range(1, groups):
        hop_copy(k, dp).wait_send()
        factor_copy(k, dp).wait_send()


def front(hidden, gain, factors, shared, mask, w_query, w_keyval, devices):
    rows, lanes = mask.shape
    groups, heads = factors.shape[:2]
    slots, width = shared.shape[1:]
    q_cols, kv_cols = w_query.shape[1], w_keyval.shape[1]
    cols = q_cols + kv_cols
    chunks = 8
    vmem = pl.BlockSpec(memory_space=pltpu.VMEM)
    anywhere = pl.BlockSpec(memory_space=pl.ANY)
    return pl.pallas_call(
        functools.partial(front_kernel, devices, groups),
        in_specs=[vmem, vmem, vmem, vmem, vmem, anywhere, anywhere],
        out_specs=[vmem, vmem, vmem],
        out_shape=[
            jax.ShapeDtypeStruct(factors.shape, BF16),
            jax.ShapeDtypeStruct((devices, groups * slots, width), BF16),
            jax.ShapeDtypeStruct((devices, rows // devices, cols), BF16),
        ],
        scratch_shapes=[
            pltpu.VMEM((chunks, D // chunks, q_cols), BF16),
            pltpu.VMEM((chunks, D // chunks, kv_cols), BF16),
            pltpu.VMEM((devices,) + hidden.shape, BF16),
            pltpu.VMEM(factors.shape, BF16),
            pltpu.VMEM((groups, slots, width), BF16),
            pltpu.VMEM((devices, groups * slots, width), BF16),
            pltpu.VMEM((rows, D), BF16),
            pltpu.VMEM((D // 2, 2 * rows), F32),
            pltpu.VMEM((J1 * rows, I1), BF16),
            pltpu.VMEM((J1, heads * rows, lanes), BF16),
            pltpu.VMEM((lanes, J1 * HD), BF16),
            pltpu.VMEM((devices, rows // devices, cols), BF16),
            pltpu.VMEM((devices, rows // devices, cols), BF16),
            pltpu.SemaphoreType.DMA((2, chunks)),
            pltpu.SemaphoreType.DMA((devices,)),
            pltpu.SemaphoreType.DMA((devices,)),
            pltpu.SemaphoreType.DMA((groups,)),
            pltpu.SemaphoreType.DMA((groups,)),
            pltpu.SemaphoreType.DMA((groups,)),
            pltpu.SemaphoreType.DMA((groups,)),
            pltpu.SemaphoreType.DMA((devices,)),
            pltpu.SemaphoreType.DMA((devices,)),
            pltpu.SemaphoreType.DMA((devices,)),
            pltpu.SemaphoreType.DMA((devices,)),
        ],
        compiler_params=params(collective_id=2, has_side_effects=True),
    )(hidden, gain.reshape(1, D), factors, shared, mask, w_query, w_keyval)


def attend_kernel(slots, length_ref, query_ref, fresh_ref, cache_ref, out_ref, held, scores, sems):
    rows, span = cache_ref.shape[0], cache_ref.shape[1]
    per_group = QH // KVH
    pieces = span // GRAIN
    coeff = 1.0 / math.sqrt(HD)

    def chunks_of(row):
        return (length_ref[row] + (GRAIN - 1)) // GRAIN

    def copy_of(row, c):
        slot = lax.rem(row, slots)
        where = pl.ds(pl.multiple_of(c * GRAIN, GRAIN), GRAIN)
        return pltpu.make_async_copy(
            cache_ref.at[row, where], held.at[slot, where], sems.at[slot, c]
        )

    def fetch(row):
        def one(c, carry):
            copy_of(row, c).start()
            return carry

        lax.fori_loop(0, chunks_of(row), one, 0)

    for row in range(min(slots - 1, rows)):
        fetch(row)

    def per_row(row, carry):
        @pl.when(row + slots - 1 < rows)
        def _():
            fetch(row + slots - 1)

        slot = lax.rem(row, slots)
        count = chunks_of(row)
        length = length_ref[row]
        query = query_ref[row]
        newest = fresh_ref[row].astype(F32)
        own_parts, value_parts = [], []
        for g in range(KVH):
            heads = slice(g * per_group, (g + 1) * per_group)
            key = newest[2 * g : 2 * g + 1]
            own_parts.append(jnp.sum(query[heads].astype(F32) * key, axis=1, keepdims=True))
            value_parts.append(jnp.broadcast_to(newest[2 * g + 1 : 2 * g + 2], (per_group, HD)))
        own = jnp.concatenate(own_parts, axis=0) * coeff
        value_new = jnp.concatenate(value_parts, axis=0)

        def finish(c, carry):
            copy_of(row, c).wait()
            return carry

        for n in range(1, pieces + 1):
            @pl.when(count == n)
            def _(n=n):
                for c in range(n):
                    finish(c, 0)
                    where = slice(c * GRAIN, (c + 1) * GRAIN)
                    for g in range(KVH):
                        heads = slice(g * per_group, (g + 1) * per_group)
                        keys = held[slot, where, 2 * g * HD : (2 * g + 1) * HD]
                        scores[heads, where] = nt_dot(query[heads], keys) * coeff
                width = n * GRAIN
                full = scores[:, :width]
                spot = lax.broadcasted_iota(jnp.int32, (QH, width), 1)
                full = jnp.where(spot < length, full, FLOOR_SCORE)
                peak = jnp.maximum(jnp.max(full, axis=1, keepdims=True), own)
                expo = jnp.exp(full - peak)
                expo_new = jnp.exp(own - peak)
                total = jnp.sum(expo, axis=1, keepdims=True) + expo_new
                weight = expo.astype(BF16)
                weight_new = expo_new.astype(BF16).astype(F32)
                summed = jnp.concatenate(
                    [
                        jnp.dot(
                            weight[g * per_group : (g + 1) * per_group],
                            held[slot, :width, (2 * g + 1) * HD : (2 * g + 2) * HD],
                            preferred_element_type=F32,
                        )
                        for g in range(KVH)
                    ],
                    axis=0,
                )
                out_ref[row] = ((summed + weight_new * value_new) / total).astype(BF16)

        return carry

    lax.fori_loop(0, rows, per_row, 0)


def attend(lengths, queries, fresh, cache):
    rows, span, width = cache.shape
    slots = min(4, rows + 1)
    return pl.pallas_call(
        functools.partial(attend_kernel, slots),
        in_specs=[
            pl.BlockSpec(memory_space=pltpu.SMEM),
            pl.BlockSpec(memory_space=pltpu.VMEM),
            pl.BlockSpec(memory_space=pltpu.VMEM),
            pl.BlockSpec(memory_space=pl.ANY),
        ],
        out_specs=pl.BlockSpec(memory_space=pltpu.VMEM),
        out_shape=jax.ShapeDtypeStruct((rows, QH, HD), BF16),
        scratch_shapes=[
            pltpu.VMEM((slots, span, width), BF16),
            pltpu.VMEM((QH, span), F32),
            pltpu.SemaphoreType.DMA((slots, span // GRAIN)),
        ],
        compiler_params=params(),
        cost_estimate=pl.CostEstimate(
            flops=4 * rows * span * QH * HD,
            bytes_accessed=rows * span * width,
            transcendentals=rows * span * QH,
        ),
    )(lengths, queries, fresh, cache)


def output_kernel(
    devices,
    att_ref,
    factor_ref,
    shared_ref,
    mask_ref,
    weight_ref,
    out_ref,
    weights,
    got_att,
    flat_att,
    turned,
    mixed,
    factors,
    spread,
    delta_rows,
    leaving,
    arriving,
    weight_sems,
    att_send,
    att_recv,
    sum_send,
    sum_recv,
):
    me = lax.axis_index("tensor")
    heads, rows_here = att_ref.shape[1], att_ref.shape[2]
    rows, lanes = mask_ref.shape
    width = weights.shape[2]
    half = I1 // 2

    def other(k):
        return lax.rem(me + k, devices)

    def weight_copy(k):
        where = pl.ds(pl.multiple_of(other(k) * width, width), width)
        return pltpu.make_async_copy(weight_ref.at[:, where], weights.at[k], weight_sems.at[k])

    def att_copy(k):
        return pltpu.make_async_remote_copy(
            src_ref=att_ref.at[other(k)],
            dst_ref=got_att.at[me],
            send_sem=att_send.at[k],
            recv_sem=att_recv.at[me],
            device_id={"tensor": other(k)},
            device_id_type=pl.DeviceIdType.MESH,
        )

    def att_arrival(k):
        return pltpu.make_async_remote_copy(
            src_ref=att_ref.at[other(k)],
            dst_ref=got_att.at[other(k)],
            send_sem=att_send.at[k],
            recv_sem=att_recv.at[other(k)],
            device_id={"tensor": other(k)},
            device_id_type=pl.DeviceIdType.MESH,
        )

    def sum_copy(k):
        return pltpu.make_async_remote_copy(
            src_ref=leaving.at[k],
            dst_ref=arriving.at[me],
            send_sem=sum_send.at[k],
            recv_sem=sum_recv.at[me],
            device_id={"tensor": other(k)},
            device_id_type=pl.DeviceIdType.MESH,
        )

    def sum_arrival(k):
        return pltpu.make_async_remote_copy(
            src_ref=leaving.at[k],
            dst_ref=arriving.at[other(k)],
            send_sem=sum_send.at[k],
            recv_sem=sum_recv.at[other(k)],
            device_id={"tensor": other(k)},
            device_id_type=pl.DeviceIdType.MESH,
        )

    barrier = pltpu.get_barrier_semaphore()
    for k in range(1, devices):
        pl.semaphore_signal(
            barrier, inc=1, device_id={"tensor": other(k)}, device_id_type=pl.DeviceIdType.MESH
        )
    order = list(range(1, devices)) + [0]
    for k in order:
        weight_copy(k).start()
    pl.semaphore_wait(barrier, devices - 1)
    for k in range(1, devices):
        att_copy(k).start()

    def store(col, size, value):
        for b in range(lanes // HD):
            turned[b, col : col + size, :] = value[b * HD : (b + 1) * HD].T

    expand_shared(shared_ref, RANK * J1 * HD, lanes, store)
    sources, depth = factor_ref.shape[0], factor_ref.shape[2]
    for h in range(heads):
        for s in range(sources):
            first = h * lanes + s * depth
            factors[first : first + depth, :] = factor_ref[s, h]
    got_att[me] = att_ref[me]
    for k in range(1, devices):
        att_arrival(k).wait_recv()

    stack = [jnp.concatenate([got_att[t, h] for t in range(devices)], axis=0) for h in range(heads)]
    for h in range(heads):
        flat_att[:, h * HD : (h + 1) * HD] = stack[h]
    stack = jnp.concatenate(stack, axis=0)
    mask = mask_ref[...]
    for j in range(J1):
        table = jnp.concatenate(
            [turned[b, pl.ds(j, HD, stride=J1), :] for b in range(lanes // HD)], axis=1
        ).astype(BF16)
        part = jnp.dot(stack, table, preferred_element_type=F32)
        for h in range(heads):
            own = jnp.where(mask > 0, part[h * rows : (h + 1) * rows], 0.0)
            mixed[j * rows : (j + 1) * rows, h * lanes : (h + 1) * lanes] = own.astype(BF16)
    for j0 in range(0, J1, 4):
        delta = jnp.dot(mixed[j0 * rows : (j0 + 4) * rows, :], factors[...], preferred_element_type=F32)
        for j in range(4):
            own = delta[j * rows : (j + 1) * rows]
            both = jnp.concatenate([own[:, :half], own[:, half:]], axis=0)
            spread[pl.ds(j0 + j, half, stride=J1), :] = both.T
    piece = D // 16
    for c in range(8):
        where = slice(c * piece, (c + 1) * piece)
        delta_rows[:, where] = spread[where, :].T

    coeff = OUT_SCALE / math.sqrt(RANK * QH * HD)
    per_half = D // 2 // width

    def partial_of(k):
        weight_copy(k).wait()
        to = other(k)
        first_row = pl.multiple_of((to // per_half) * rows, rows)
        first_col = pl.multiple_of(lax.rem(to, per_half) * width, width)
        base = jnp.dot(flat_att[...], weights[k], preferred_element_type=F32)
        delta = delta_rows[pl.ds(first_row, rows), pl.ds(first_col, width)]
        return (base + coeff * delta).astype(BF16)

    def send_one(k, carry):
        leaving[k] = partial_of(k)
        sum_copy(k).start()
        return carry

    lax.fori_loop(1, devices, send_one, 0)
    total = partial_of(0).astype(F32)
    for k in range(1, devices):
        sum_arrival(k).wait_recv()
        total += arriving[other(k)].astype(F32)
    out_ref[...] = total.astype(BF16)
    for k in range(1, devices):
        att_copy(k).wait_send()
        sum_copy(k).wait_send()


def project_out(attended, factors, shared, mask, w_out):
    devices, heads, rows_here, _ = attended.shape
    rows, lanes = mask.shape
    inner = heads * HD
    width = D // devices
    vmem = pl.BlockSpec(memory_space=pltpu.VMEM)
    return pl.pallas_call(
        functools.partial(output_kernel, devices),
        in_specs=[vmem, vmem, vmem, vmem, pl.BlockSpec(memory_space=pl.ANY)],
        out_specs=vmem,
        out_shape=jax.ShapeDtypeStruct((rows, width), BF16),
        scratch_shapes=[
            pltpu.VMEM((devices, inner, width), BF16),
            pltpu.VMEM((devices, heads, rows_here, HD), BF16),
            pltpu.VMEM((rows, inner), BF16),
            pltpu.VMEM((lanes // HD, J1 * HD, HD), F32),
            pltpu.VMEM((J1 * rows, heads * lanes), BF16),
            pltpu.VMEM((heads * lanes, I1), BF16),
            pltpu.VMEM((D // 2, 2 * rows), F32),
            pltpu.VMEM((2 * rows, D // 2), F32),
            pltpu.VMEM((devices, rows, width), BF16),
            pltpu.VMEM((devices, rows, width), BF16),
            pltpu.SemaphoreType.DMA((devices,)),
            pltpu.SemaphoreType.DMA((devices,)),
            pltpu.SemaphoreType.DMA((devices,)),
            pltpu.SemaphoreType.DMA((devices,)),
            pltpu.SemaphoreType.DMA((devices,)),
        ],
        compiler_params=params(collective_id=1, has_side_effects=True),
    )(attended, factors, shared, mask, w_out)


def on_device(
    hidden_in,
    norm_gain,
    w_query,
    w_keyval,
    w_out,
    kv_cache,
    cache_length,
    row_tenant,
    tenant_lists,
    adapter_heads,
    adapter_shared,
):
    groups, slots = tenant_lists.shape[0], tenant_lists.shape[2]
    stored, heads_here = adapter_heads.shape[:2]
    dp = lax.axis_index("dp")
    outgoing = lax.dynamic_index_in_dim(tenant_lists, dp, 0, keepdims=False).reshape(-1)

    picker = (outgoing[:, None] == jnp.arange(stored, dtype=jnp.int32)[None, :]).astype(BF16)
    send_shared = (
        jnp.dot(picker, adapter_shared, preferred_element_type=F32)
        .astype(BF16)
        .reshape(groups, slots, adapter_shared.shape[1])
    )
    lanes = groups * slots * RANK * 2
    picked = pick_tenants(jnp.maximum(outgoing, 0), adapter_heads)
    picked = picked.reshape(groups, slots, heads_here, RANK * 2, I1).transpose(0, 2, 1, 3, 4)
    picked = picked.reshape(groups, heads_here, slots * RANK * 2, I1)

    incoming = lax.dynamic_index_in_dim(tenant_lists, dp, 1, keepdims=False)
    ids = jnp.where(incoming >= 0, jnp.arange(groups, dtype=jnp.int32)[:, None] * stored + incoming, -1)
    ids = jnp.repeat(ids.reshape(-1), RANK * 2)
    own = row_tenant[:, None] == ids[None, :]
    part = jnp.arange(lanes, dtype=jnp.int32)[None, :] % 2
    mask_query = (own & (part == 0)).astype(F32)
    mask_out = (own & (part == 1)).astype(F32)

    devices = QH // heads_here
    factors, shared, parts = front(
        hidden_in, norm_gain, picked, send_shared, mask_query, w_query, w_keyval, devices
    )
    rows_here, span, width = kv_cache.shape[1:]
    q_cols = heads_here * HD
    queries = parts[:, :, :q_cols].transpose(1, 0, 2).reshape(rows_here, QH, HD)
    fresh = parts[:, :, q_cols:].transpose(1, 0, 2).reshape(rows_here, 2 * KVH, HD)
    first_row = lax.axis_index("tensor") * rows_here
    lengths = lax.dynamic_slice_in_dim(cache_length, first_row, rows_here, 0)
    attended = attend(lengths, queries, fresh, kv_cache.reshape(rows_here, span, width))
    attended = attended.reshape(rows_here, devices, heads_here, HD).transpose(1, 2, 0, 3)
    return project_out(attended, factors, shared, mask_out, w_out)


def solution(mesh):
    placed = (
        P(("groups", "dp"), "tensor"),
        P(),
        P(None, "tensor"),
        P(None, "tensor"),
        P("tensor", None),
        P(("groups", "dp"), "tensor", None, None),
        P(("groups", "dp")),
        P(("groups", "dp")),
        P("groups", None, None),
        P("dp", "tensor", None, None, None),
        P("dp", "tensor"),
    )
    return jax.shard_map(
        on_device,
        mesh=mesh,
        in_specs=placed,
        out_specs=P(("groups", "dp"), "tensor"),
        check_vma=False,
    )
```

```python
import functools
import math

import jax
import jax.numpy as jnp
from jax import lax
from jax.experimental import pallas as pl
from jax.experimental.pallas import tpu as pltpu
from jax.sharding import PartitionSpec as P

D = 8192
QH = 32
KVH = 4
HD = 128
I1 = 512
J1 = 16
RANK = 4
FLOOR_SCORE = -1e30
OUT_SCALE = 8.0
GRAIN = 256
F32 = jnp.float32
BF16 = jnp.bfloat16
VMEM_BYTES = 56 * 1024 * 1024


def params(**more):
    return pltpu.CompilerParams(vmem_limit_bytes=VMEM_BYTES, **more)


def nt_dot(left, right):
    return lax.dot_general(left, right, (((1,), (1,)), ((), ())), preferred_element_type=F32)


def pick_kernel(count, index_ref, store_ref, out_ref, sems):
    for k in range(count):
        pltpu.make_async_copy(store_ref.at[index_ref[k]], out_ref.at[k], sems.at[k]).start()
    for k in range(count):
        pltpu.make_async_copy(store_ref.at[index_ref[k]], out_ref.at[k], sems.at[k]).wait()


def pick_tenants(indices, store):
    count = indices.shape[0]
    return pl.pallas_call(
        functools.partial(pick_kernel, count),
        in_specs=[
            pl.BlockSpec(memory_space=pltpu.SMEM),
            pl.BlockSpec(memory_space=pl.ANY),
        ],
        out_specs=pl.BlockSpec(memory_space=pltpu.VMEM),
        scratch_shapes=[pltpu.SemaphoreType.DMA((count,))],
        out_shape=jax.ShapeDtypeStruct((count,) + store.shape[1:], store.dtype),
        compiler_params=params(),
    )(indices, store)


def mesh_copy(source, target, send_sem, recv_sem, axis, place):
    return pltpu.make_async_remote_copy(
        src_ref=source,
        dst_ref=target,
        send_sem=send_sem,
        recv_sem=recv_sem,
        device_id={axis: place},
        device_id_type=pl.DeviceIdType.MESH,
    )


def stack_factors(factors, head):
    sources, slots = factors.shape[:2]
    pieces = [factors[s, k, head].astype(F32) for s in range(sources) for k in range(slots)]
    return jnp.concatenate(pieces, axis=0).astype(BF16)


class Line:
    def __init__(self, devices, me, buffer, send, recv):
        self.devices, self.me, self.buffer, self.send, self.recv = devices, me, buffer, send, recv

    def copy(self, source, side, hop):
        step = 1 if side == 0 else -1
        place = lax.rem(self.me + step + self.devices, self.devices)
        block = self.buffer.at[source]
        return mesh_copy(block, block, self.send.at[side, hop], self.recv.at[source], "tensor", place)

    def legs(self, hop):
        for side in range(2):
            source = self.me - hop if side == 0 else self.me + hop
            there = source >= 0 if side == 0 else source < self.devices
            more = self.me + 1 < self.devices if side == 0 else self.me >= 1
            yield side, source, there, there & more

    def move(self, hop):
        for side, source, there, onward in self.legs(hop):
            if hop:
                @pl.when(there)
                def _(side=side, source=source):
                    self.copy(source, side, hop).wait_recv()

            @pl.when(onward)
            def _(side=side, source=source):
                self.copy(source, side, hop).start()

    def finish(self):
        for hop in range(self.devices - 1):
            for side, source, _, onward in self.legs(hop):
                @pl.when(onward)
                def _(side=side, source=source, hop=hop):
                    self.copy(source, side, hop).wait_send()


def expand_shared(blocks, first, lanes, store):
    tenants, width = blocks.shape[1], blocks.shape[2]
    span = J1 * HD
    piece = min(width, span)
    lane = lax.broadcasted_iota(jnp.int32, (lanes, RANK * tenants), 0)
    entry = lax.broadcasted_iota(jnp.int32, (lanes, RANK * tenants), 1)
    wanted = (lane // 2) % RANK * tenants + lane // (2 * RANK)
    chooser = (wanted == entry).astype(F32).astype(BF16)
    for col in range(0, span, piece):
        stack = []
        for r in range(RANK):
            start = first + r * span + col
            local = start % width
            stack.append(blocks[start // width, :, local : local + piece])
        stack = jnp.concatenate(stack, axis=0)
        store(col, piece, jnp.dot(chooser, stack, preferred_element_type=F32))


def front_kernel(
    devices,
    groups,
    hidden_ref,
    gain_ref,
    factor_ref,
    shared_ref,
    mask_ref,
    wq_ref,
    wkv_ref,
    factors_out,
    shared_out,
    rows_out,
    wq,
    wkv,
    hidden,
    factors,
    first_hop,
    blocks,
    normed,
    turned,
    spread,
    inner,
    table,
    leaving,
    arriving,
    weight_sems,
    hidden_send,
    hidden_recv,
    factor_send,
    factor_recv,
    hop_send,
    hop_recv,
    block_send,
    block_recv,
    row_send,
    row_recv,
):
    me, dp = lax.axis_index("tensor"), lax.axis_index("dp")
    rows, lanes = mask_ref.shape
    heads = factor_ref.shape[2]
    width = hidden_ref.shape[1]
    chunks, depth = wq.shape[0], wq.shape[1]
    rows_here = arriving.shape[1]
    q_cols = wq.shape[2]

    def peer(k):
        return lax.rem(me + k, devices)

    def mate(k):
        return lax.rem(dp + k, groups)

    def weight_copies(c):
        where = pl.ds(c * depth, depth)
        return (
            pltpu.make_async_copy(wq_ref.at[where], wq.at[c], weight_sems.at[0, c]),
            pltpu.make_async_copy(wkv_ref.at[where], wkv.at[c], weight_sems.at[1, c]),
        )

    features = Line(devices, me, hidden, hidden_send, hidden_recv)
    shares = Line(devices, me, blocks, block_send, block_recv)

    def row_copy(k, to):
        return mesh_copy(leaving.at[peer(k)], arriving.at[to], row_send.at[k], row_recv.at[to], "tensor", peer(k))

    def hop_copy(k, to):
        return mesh_copy(shared_ref.at[mate(k)], first_hop.at[to], hop_send.at[k], hop_recv.at[to], "dp", mate(k))

    def factor_copy(k, to):
        return mesh_copy(factor_ref.at[mate(k)], factors.at[to], factor_send.at[k], factor_recv.at[to], "dp", mate(k))

    barrier = pltpu.get_barrier_semaphore()
    for k in range(1, devices):
        pl.semaphore_signal(barrier, inc=1, device_id={"tensor": peer(k)}, device_id_type=pl.DeviceIdType.MESH)
    for k in range(1, groups):
        pl.semaphore_signal(barrier, inc=1, device_id={"dp": mate(k)}, device_id_type=pl.DeviceIdType.MESH)
    for c in range(chunks):
        for copy in weight_copies(c):
            copy.start()
    pl.semaphore_wait(barrier, devices - 1 + groups - 1)
    for k in range(1, groups):
        hop_copy(k, dp).start()
    hidden[me] = hidden_ref[...]
    features.move(0)
    for k in range(1, groups):
        factor_copy(k, dp).start()
    first_hop[dp] = shared_ref[dp]
    factors[dp] = factor_ref[dp]
    for k in range(1, groups):
        hop_copy(k, mate(k)).wait_recv()
    blocks[me] = jnp.concatenate([first_hop[s].astype(F32) for s in range(groups)], axis=0).astype(BF16)
    for hop in range(1, devices):
        features.move(hop)
        if hop == 1:
            shares.move(0)
    squares = jnp.zeros((rows, 1), F32)
    for t in range(devices):
        wide = hidden[t].astype(F32)
        squares += jnp.sum(wide * wide, axis=1, keepdims=True)
    inverse = lax.rsqrt(squares / D + 1e-05)
    for t in range(devices):
        where = slice(t * width, (t + 1) * width)
        normed[:, where] = (hidden[t].astype(F32) * inverse * gain_ref[:, where].astype(F32)).astype(BF16)
    base = jnp.zeros((rows, q_cols), F32)
    keyval = jnp.zeros((rows, wkv.shape[2]), F32)
    for c in range(chunks):
        for copy in weight_copies(c):
            copy.wait()
        part = normed[:, c * depth : (c + 1) * depth]
        base += jnp.dot(part, wq[c], preferred_element_type=F32)
        keyval += jnp.dot(part, wkv[c], preferred_element_type=F32)

    shares.move(1)
    half = D // 2
    piece = half // 4
    for c in range(4):
        both = jnp.concatenate(
            [normed[:, c * piece : (c + 1) * piece], normed[:, half + c * piece : half + (c + 1) * piece]],
            axis=0,
        ).astype(F32)
        turned[c * piece : (c + 1) * piece, :] = both.T
    for j in range(J1):
        back = turned[pl.ds(j, I1 // 2, stride=J1), :].T
        spread[j * rows : (j + 1) * rows, : I1 // 2] = back[:rows].astype(BF16)
        spread[j * rows : (j + 1) * rows, I1 // 2 :] = back[rows:].astype(BF16)

    if devices > 2:
        shares.move(2)
    for k in range(1, groups):
        factor_copy(k, mate(k)).wait_recv()
    mask = mask_ref[...]
    for h in range(heads):
        factor = stack_factors(factors, h)
        for j0 in range(0, J1, 4):
            part = nt_dot(spread[j0 * rows : (j0 + 4) * rows, :], factor)
            for j in range(4):
                own = jnp.where(mask > 0, part[j * rows : (j + 1) * rows], 0.0)
                inner[j0 + j, h * rows : (h + 1) * rows, :] = own.astype(BF16)
    factors_out[...] = factors[...]

    for hop in range(3, devices):
        shares.move(hop)

    def store(col, size, value):
        table[:, col : col + size] = value.astype(BF16)

    expand_shared(blocks, 0, lanes, store)
    shared_out[...] = blocks[...]
    delta = jnp.zeros((heads * rows, HD), F32)
    for j in range(J1):
        delta += jnp.dot(inner[j], table[:, j * HD : (j + 1) * HD], preferred_element_type=F32)
    coeff = 1.0 / math.sqrt(RANK * D)
    query = jnp.concatenate(
        [base[:, h * HD : (h + 1) * HD] + coeff * delta[h * rows : (h + 1) * rows] for h in range(heads)], axis=1
    )
    for t in range(devices):
        where = slice(t * rows_here, (t + 1) * rows_here)
        leaving[t, :, :q_cols] = query[where].astype(BF16)
        leaving[t, :, q_cols:] = keyval[where].astype(BF16)
    for k in range(1, devices):
        row_copy(k, me).start()
    arriving[me] = leaving[me]
    for k in range(1, devices):
        row_copy(k, peer(k)).wait_recv()
    rows_out[...] = arriving[...]
    for k in range(1, devices):
        row_copy(k, me).wait_send()
    features.finish()
    shares.finish()
    for k in range(1, groups):
        hop_copy(k, dp).wait_send()
        factor_copy(k, dp).wait_send()


def front(hidden, gain, factors, shared, mask, w_query, w_keyval, devices):
    rows, lanes = mask.shape
    groups = factors.shape[0]
    slots, width = shared.shape[1:]
    q_cols, kv_cols = w_query.shape[1], w_keyval.shape[1]
    cols = q_cols + kv_cols
    chunks = 8
    vmem = pl.BlockSpec(memory_space=pltpu.VMEM)
    anywhere = pl.BlockSpec(memory_space=pl.ANY)
    return pl.pallas_call(
        functools.partial(front_kernel, devices, groups),
        in_specs=[vmem, vmem, vmem, vmem, vmem, anywhere, anywhere],
        out_specs=[vmem, vmem, vmem],
        out_shape=[
            jax.ShapeDtypeStruct(factors.shape, BF16),
            jax.ShapeDtypeStruct((devices, groups * slots, width), BF16),
            jax.ShapeDtypeStruct((devices, rows // devices, cols), BF16),
        ],
        scratch_shapes=[
            pltpu.VMEM((chunks, D // chunks, q_cols), BF16),
            pltpu.VMEM((chunks, D // chunks, kv_cols), BF16),
            pltpu.VMEM((devices,) + hidden.shape, BF16),
            pltpu.VMEM(factors.shape, BF16),
            pltpu.VMEM((groups, slots, width), BF16),
            pltpu.VMEM((devices, groups * slots, width), BF16),
            pltpu.VMEM((rows, D), BF16),
            pltpu.VMEM((D // 2, 2 * rows), F32),
            pltpu.VMEM((J1 * rows, I1), BF16),
            pltpu.VMEM((J1, factors.shape[2] * rows, lanes), BF16),
            pltpu.VMEM((lanes, J1 * HD), BF16),
            pltpu.VMEM((devices, rows // devices, cols), BF16),
            pltpu.VMEM((devices, rows // devices, cols), BF16),
            pltpu.SemaphoreType.DMA((2, chunks)),
            pltpu.SemaphoreType.DMA((2, devices)),
            pltpu.SemaphoreType.DMA((devices,)),
            pltpu.SemaphoreType.DMA((groups,)),
            pltpu.SemaphoreType.DMA((groups,)),
            pltpu.SemaphoreType.DMA((groups,)),
            pltpu.SemaphoreType.DMA((groups,)),
            pltpu.SemaphoreType.DMA((2, devices)),
            pltpu.SemaphoreType.DMA((devices,)),
            pltpu.SemaphoreType.DMA((devices,)),
            pltpu.SemaphoreType.DMA((devices,)),
        ],
        compiler_params=params(collective_id=2, has_side_effects=True),
    )(hidden, gain.reshape(1, D), factors, shared, mask, w_query, w_keyval)


def attend_kernel(slots, length_ref, query_ref, fresh_ref, cache_ref, out_ref, held, scores, sems):
    rows, span = cache_ref.shape[0], cache_ref.shape[1]
    per_group = QH // KVH
    pieces = span // GRAIN
    coeff = 1.0 / math.sqrt(HD)

    def chunks_of(row):
        return (length_ref[row] + (GRAIN - 1)) // GRAIN

    def copy_of(row, c):
        slot = lax.rem(row, slots)
        where = pl.ds(pl.multiple_of(c * GRAIN, GRAIN), GRAIN)
        return pltpu.make_async_copy(
            cache_ref.at[row, where], held.at[slot, where], sems.at[slot, c]
        )

    def fetch(row):
        def one(c, carry):
            copy_of(row, c).start()
            return carry

        lax.fori_loop(0, chunks_of(row), one, 0)

    for row in range(min(slots - 1, rows)):
        fetch(row)

    def per_row(row, carry):
        @pl.when(row + slots - 1 < rows)
        def _():
            fetch(row + slots - 1)

        slot = lax.rem(row, slots)
        count = chunks_of(row)
        length = length_ref[row]
        query = query_ref[row]
        newest = fresh_ref[row].astype(F32)
        own_parts, value_parts = [], []
        for g in range(KVH):
            heads = slice(g * per_group, (g + 1) * per_group)
            key = newest[2 * g : 2 * g + 1]
            own_parts.append(jnp.sum(query[heads].astype(F32) * key, axis=1, keepdims=True))
            value_parts.append(jnp.broadcast_to(newest[2 * g + 1 : 2 * g + 2], (per_group, HD)))
        own = jnp.concatenate(own_parts, axis=0) * coeff
        value_new = jnp.concatenate(value_parts, axis=0)

        def finish(c, carry):
            copy_of(row, c).wait()
            return carry

        for n in range(1, pieces + 1):
            @pl.when(count == n)
            def _(n=n):
                for c in range(n):
                    finish(c, 0)
                    where = slice(c * GRAIN, (c + 1) * GRAIN)
                    for g in range(KVH):
                        heads = slice(g * per_group, (g + 1) * per_group)
                        keys = held[slot, where, 2 * g * HD : (2 * g + 1) * HD]
                        scores[heads, where] = nt_dot(query[heads], keys) * coeff
                width = n * GRAIN
                full = scores[:, :width]
                spot = lax.broadcasted_iota(jnp.int32, (QH, width), 1)
                full = jnp.where(spot < length, full, FLOOR_SCORE)
                peak = jnp.maximum(jnp.max(full, axis=1, keepdims=True), own)
                expo = jnp.exp(full - peak)
                expo_new = jnp.exp(own - peak)
                total = jnp.sum(expo, axis=1, keepdims=True) + expo_new
                weight = expo.astype(BF16)
                weight_new = expo_new.astype(BF16).astype(F32)
                summed = jnp.concatenate(
                    [
                        jnp.dot(
                            weight[g * per_group : (g + 1) * per_group],
                            held[slot, :width, (2 * g + 1) * HD : (2 * g + 2) * HD],
                            preferred_element_type=F32,
                        )
                        for g in range(KVH)
                    ],
                    axis=0,
                )
                out_ref[row] = ((summed + weight_new * value_new) / total).astype(BF16)

        return carry

    lax.fori_loop(0, rows, per_row, 0)


def attend(lengths, queries, fresh, cache):
    rows, span, width = cache.shape
    slots = min(4, rows + 1)
    return pl.pallas_call(
        functools.partial(attend_kernel, slots),
        in_specs=[
            pl.BlockSpec(memory_space=pltpu.SMEM),
            pl.BlockSpec(memory_space=pltpu.VMEM),
            pl.BlockSpec(memory_space=pltpu.VMEM),
            pl.BlockSpec(memory_space=pl.ANY),
        ],
        out_specs=pl.BlockSpec(memory_space=pltpu.VMEM),
        out_shape=jax.ShapeDtypeStruct((rows, QH, HD), BF16),
        scratch_shapes=[
            pltpu.VMEM((slots, span, width), BF16),
            pltpu.VMEM((QH, span), F32),
            pltpu.SemaphoreType.DMA((slots, span // GRAIN)),
        ],
        compiler_params=params(),
        cost_estimate=pl.CostEstimate(
            flops=4 * rows * span * QH * HD,
            bytes_accessed=rows * span * width,
            transcendentals=rows * span * QH,
        ),
    )(lengths, queries, fresh, cache)


def output_kernel(
    devices,
    att_ref,
    factor_ref,
    shared_ref,
    mask_ref,
    weight_ref,
    out_ref,
    weights,
    got_att,
    flat_att,
    turned,
    mixed,
    factors,
    spread,
    delta_rows,
    leaving,
    arriving,
    weight_sems,
    att_send,
    att_recv,
    sum_send,
    sum_recv,
):
    me = lax.axis_index("tensor")
    heads, rows_here = att_ref.shape[1], att_ref.shape[2]
    rows, lanes = mask_ref.shape
    width = weights.shape[2]
    half = I1 // 2

    def other(k):
        return lax.rem(me + k, devices)

    def weight_copy(k):
        where = pl.ds(pl.multiple_of(other(k) * width, width), width)
        return pltpu.make_async_copy(weight_ref.at[:, where], weights.at[k], weight_sems.at[k])

    def att_copy(k):
        return pltpu.make_async_remote_copy(
            src_ref=att_ref.at[other(k)],
            dst_ref=got_att.at[me],
            send_sem=att_send.at[k],
            recv_sem=att_recv.at[me],
            device_id={"tensor": other(k)},
            device_id_type=pl.DeviceIdType.MESH,
        )

    def att_arrival(k):
        return pltpu.make_async_remote_copy(
            src_ref=att_ref.at[other(k)],
            dst_ref=got_att.at[other(k)],
            send_sem=att_send.at[k],
            recv_sem=att_recv.at[other(k)],
            device_id={"tensor": other(k)},
            device_id_type=pl.DeviceIdType.MESH,
        )

    def sum_copy(k):
        return pltpu.make_async_remote_copy(
            src_ref=leaving.at[k],
            dst_ref=arriving.at[me],
            send_sem=sum_send.at[k],
            recv_sem=sum_recv.at[me],
            device_id={"tensor": other(k)},
            device_id_type=pl.DeviceIdType.MESH,
        )

    def sum_arrival(k):
        return pltpu.make_async_remote_copy(
            src_ref=leaving.at[k],
            dst_ref=arriving.at[other(k)],
            send_sem=sum_send.at[k],
            recv_sem=sum_recv.at[other(k)],
            device_id={"tensor": other(k)},
            device_id_type=pl.DeviceIdType.MESH,
        )

    barrier = pltpu.get_barrier_semaphore()
    for k in range(1, devices):
        pl.semaphore_signal(
            barrier, inc=1, device_id={"tensor": other(k)}, device_id_type=pl.DeviceIdType.MESH
        )
    order = list(range(1, devices)) + [0]
    for k in order:
        weight_copy(k).start()
    pl.semaphore_wait(barrier, devices - 1)
    for k in range(1, devices):
        att_copy(k).start()

    def store(col, size, value):
        for b in range(lanes // HD):
            turned[b, col : col + size, :] = value[b * HD : (b + 1) * HD].T

    expand_shared(shared_ref, RANK * J1 * HD, lanes, store)
    for h in range(heads):
        factors[h * lanes : (h + 1) * lanes, :] = stack_factors(factor_ref, h)
    got_att[me] = att_ref[me]
    for k in range(1, devices):
        att_arrival(k).wait_recv()

    stack = [jnp.concatenate([got_att[t, h] for t in range(devices)], axis=0) for h in range(heads)]
    for h in range(heads):
        flat_att[:, h * HD : (h + 1) * HD] = stack[h]
    stack = jnp.concatenate(stack, axis=0)
    mask = mask_ref[...]
    for j in range(J1):
        table = jnp.concatenate(
            [turned[b, pl.ds(j, HD, stride=J1), :] for b in range(lanes // HD)], axis=1
        ).astype(BF16)
        part = jnp.dot(stack, table, preferred_element_type=F32)
        for h in range(heads):
            own = jnp.where(mask > 0, part[h * rows : (h + 1) * rows], 0.0)
            mixed[j * rows : (j + 1) * rows, h * lanes : (h + 1) * lanes] = own.astype(BF16)
    for j0 in range(0, J1, 4):
        delta = jnp.dot(mixed[j0 * rows : (j0 + 4) * rows, :], factors[...], preferred_element_type=F32)
        for j in range(4):
            own = delta[j * rows : (j + 1) * rows]
            both = jnp.concatenate([own[:, :half], own[:, half:]], axis=0)
            spread[pl.ds(j0 + j, half, stride=J1), :] = both.T
    piece = D // 16
    for c in range(8):
        where = slice(c * piece, (c + 1) * piece)
        delta_rows[:, where] = spread[where, :].T

    coeff = OUT_SCALE / math.sqrt(RANK * QH * HD)
    per_half = D // 2 // width

    def partial_of(k):
        weight_copy(k).wait()
        to = other(k)
        first_row = pl.multiple_of((to // per_half) * rows, rows)
        first_col = pl.multiple_of(lax.rem(to, per_half) * width, width)
        base = jnp.dot(flat_att[...], weights[k], preferred_element_type=F32)
        delta = delta_rows[pl.ds(first_row, rows), pl.ds(first_col, width)]
        return (base + coeff * delta).astype(BF16)

    def send_one(k, carry):
        leaving[k] = partial_of(k)
        sum_copy(k).start()
        return carry

    lax.fori_loop(1, devices, send_one, 0)
    total = partial_of(0).astype(F32)
    for k in range(1, devices):
        sum_arrival(k).wait_recv()
        total += arriving[other(k)].astype(F32)
    out_ref[...] = total.astype(BF16)
    for k in range(1, devices):
        att_copy(k).wait_send()
        sum_copy(k).wait_send()


def project_out(attended, factors, shared, mask, w_out):
    devices, heads, rows_here, _ = attended.shape
    rows, lanes = mask.shape
    inner = heads * HD
    width = D // devices
    vmem = pl.BlockSpec(memory_space=pltpu.VMEM)
    return pl.pallas_call(
        functools.partial(output_kernel, devices),
        in_specs=[vmem, vmem, vmem, vmem, pl.BlockSpec(memory_space=pl.ANY)],
        out_specs=vmem,
        out_shape=jax.ShapeDtypeStruct((rows, width), BF16),
        scratch_shapes=[
            pltpu.VMEM((devices, inner, width), BF16),
            pltpu.VMEM((devices, heads, rows_here, HD), BF16),
            pltpu.VMEM((rows, inner), BF16),
            pltpu.VMEM((lanes // HD, J1 * HD, HD), F32),
            pltpu.VMEM((J1 * rows, heads * lanes), BF16),
            pltpu.VMEM((heads * lanes, I1), BF16),
            pltpu.VMEM((D // 2, 2 * rows), F32),
            pltpu.VMEM((2 * rows, D // 2), F32),
            pltpu.VMEM((devices, rows, width), BF16),
            pltpu.VMEM((devices, rows, width), BF16),
            pltpu.SemaphoreType.DMA((devices,)),
            pltpu.SemaphoreType.DMA((devices,)),
            pltpu.SemaphoreType.DMA((devices,)),
            pltpu.SemaphoreType.DMA((devices,)),
            pltpu.SemaphoreType.DMA((devices,)),
        ],
        compiler_params=params(collective_id=1, has_side_effects=True),
    )(attended, factors, shared, mask, w_out)


def on_device(
    hidden_in,
    norm_gain,
    w_query,
    w_keyval,
    w_out,
    kv_cache,
    cache_length,
    row_tenant,
    tenant_lists,
    adapter_heads,
    adapter_shared,
):
    groups, slots = tenant_lists.shape[0], tenant_lists.shape[2]
    stored, heads_here = adapter_heads.shape[:2]
    dp = lax.axis_index("dp")
    outgoing = lax.dynamic_index_in_dim(tenant_lists, dp, 0, keepdims=False).reshape(-1)

    picker = (outgoing[:, None] == jnp.arange(stored, dtype=jnp.int32)[None, :]).astype(BF16)
    send_shared = (
        jnp.dot(picker, adapter_shared, preferred_element_type=F32)
        .astype(BF16)
        .reshape(groups, slots, adapter_shared.shape[1])
    )
    lanes = groups * slots * RANK * 2
    picked = pick_tenants(jnp.maximum(outgoing, 0), adapter_heads)
    picked = picked.reshape(groups, slots, heads_here, RANK * 2, I1)

    incoming = lax.dynamic_index_in_dim(tenant_lists, dp, 1, keepdims=False)
    ids = jnp.where(incoming >= 0, jnp.arange(groups, dtype=jnp.int32)[:, None] * stored + incoming, -1)
    ids = jnp.repeat(ids.reshape(-1), RANK * 2)
    own = row_tenant[:, None] == ids[None, :]
    part = jnp.arange(lanes, dtype=jnp.int32)[None, :] % 2
    mask_query = (own & (part == 0)).astype(F32)
    mask_out = (own & (part == 1)).astype(F32)

    devices = QH // heads_here
    factors, shared, parts = front(
        hidden_in, norm_gain, picked, send_shared, mask_query, w_query, w_keyval, devices
    )
    rows_here, span, width = kv_cache.shape[1:]
    q_cols = heads_here * HD
    queries = parts[:, :, :q_cols].transpose(1, 0, 2).reshape(rows_here, QH, HD)
    fresh = parts[:, :, q_cols:].transpose(1, 0, 2).reshape(rows_here, 2 * KVH, HD)
    first_row = lax.axis_index("tensor") * rows_here
    lengths = lax.dynamic_slice_in_dim(cache_length, first_row, rows_here, 0)
    attended = attend(lengths, queries, fresh, kv_cache.reshape(rows_here, span, width))
    attended = attended.reshape(rows_here, devices, heads_here, HD).transpose(1, 2, 0, 3)
    return project_out(attended, factors, shared, mask_out, w_out)


def solution(mesh):
    placed = (
        P(("groups", "dp"), "tensor"),
        P(),
        P(None, "tensor"),
        P(None, "tensor"),
        P("tensor", None),
        P(("groups", "dp"), "tensor", None, None),
        P(("groups", "dp")),
        P(("groups", "dp")),
        P("groups", None, None),
        P("dp", "tensor", None, None, None),
        P("dp", "tensor"),
    )
    return jax.shard_map(
        on_device,
        mesh=mesh,
        in_specs=placed,
        out_specs=P(("groups", "dp"), "tensor"),
        check_vma=False,
    )
```
